512 devices in a mesh: dir: 4 (over x), tex: 128 (over z, y, core).
Axes of the slice: x: 4, y: 4, z: 16, core: 2. Of those that a mesh axis runs over, the one named last changes fastest.
Arguments:
- slab: bfloat16 [131072, 4096], P('tex', 'dir'), may hold values from -4 to 4
- exponents: int32 [1024, 32], P('tex', 'dir'), may hold values from -2 to 2
- sketch: bfloat16 [4096, 512], P('dir'), may hold values from -0.09375 to 0.09375
Outputs:
- basis: bfloat16 [131072, 512], P(('tex', 'dir'))
The draws below stay inside these ranges and needn't reach their ends.
All inputs are finite; a program needn't handle non-finite values.
Results may differ from the reference program's by a relative error of at most 0.02.
Values may be sent and summed in bfloat16 or wider, within the bound.
No kernel may reach another device: no remote copies, remote signals or barrier semaphores. Data moves between devices by JAX's collectives and lax.ppermute only.
A program may use at most 64 MiB of HBM per device.

```python
import math
import jax
import jax.numpy as jnp
from jax import lax

R = 512
BLOCK = 128
DIR_DEV = 1024
TEX_DEV = 1024
TEXELS = 131072
DIRS = 4096
N_DIR = 4
N_TEX = 128


def draw_exponents(key, part):
    key = jax.random.fold_in(key, 7)
    row_blocks = TEXELS // BLOCK
    col_blocks = DIRS // BLOCK
    group_blocks = TEX_DEV // BLOCK
    inside = jnp.arange(row_blocks, dtype=jnp.int32) % group_blocks
    rising = 3 * inside // group_blocks - 1
    noise = jax.random.randint(key, (row_blocks, col_blocks), -1, 2, dtype=jnp.int32)
    return (rising[:, None] + noise).astype(jnp.int32)


def steps_of(own_key, shape, shards, low, largest):
    loudness = 1.0
    for axis_at, parts in shards:
        heights = jax.random.uniform(jax.random.fold_in(jax.random.fold_in(own_key, 6), axis_at), (parts,), jnp.float32, low / len(shards), largest / len(shards))
        loudness = loudness * jnp.repeat(jnp.exp(heights), shape[axis_at] // parts).reshape((-1,) + (1,) * (len(shape) - 1 - axis_at))
    return loudness


def bell_draw(stream_key, shape, deviation, bound, shards=(), kind=jnp.bfloat16):
    factor_of = steps_of(stream_key, shape, shards, -0.22, 0.18) if shards else 1.0
    entries = jax.random.normal(stream_key, shape, jnp.float32) * deviation * factor_of
    return jnp.minimum(jnp.maximum(entries, -bound), bound).astype(kind)


def setup_inputs(seed: int = 0) -> dict:
    splits = jax.random.split(jax.random.key(seed), 4)
    slab = bell_draw(splits[0], (TEXELS, DIRS), 1.0, 4.0, ((0, 128), (1, 4)))
    exponents = draw_exponents(jax.random.fold_in(splits[3], 71), 0)
    sketch = bell_draw(splits[2], (DIRS, R), DIRS ** -0.5, 0.09375, ((0, 4),))
    return {"slab": slab, "exponents": exponents, "sketch": sketch}


def scales_of(exponent_table):
    total = jnp.zeros(exponent_table.shape, jnp.float32)
    for exponent_value in range(-2, 3):
        total = total + jnp.where(exponent_table == exponent_value, jnp.float32(2.0 ** exponent_value), jnp.float32(0.0))
    return total.astype(jnp.bfloat16)

def dequantize(values, exponent_table):
    height, breadth = values.shape
    edge_rows = height // exponent_table.shape[0]
    edge_cols = breadth // exponent_table.shape[1]
    scale_table = scales_of(exponent_table)
    tiled = values.reshape(exponent_table.shape[0], edge_rows, exponent_table.shape[1], edge_cols)
    tiled = tiled * scale_table[:, None, :, None]
    return tiled.reshape(height, breadth)

def sketch_group(operands, sketch):
    group_values, group_exponents = operands
    scaled_values = dequantize(group_values, group_exponents)
    height = scaled_values.shape[0]
    pieces = scaled_values.reshape(height, N_DIR, DIR_DEV).astype(jnp.float32)
    sketch_blocks = sketch.reshape(N_DIR, DIR_DEV, R).astype(jnp.float32)
    partial_value = jnp.einsum('rdk,dkc->drc', pieces, sketch_blocks, precision=lax.Precision.HIGHEST)
    rounded = lax.optimization_barrier(partial_value.astype(jnp.bfloat16))
    return lax.optimization_barrier(jnp.sum(rounded.astype(jnp.float32), axis=0))

def column_gram(matrix):
    return lax.dot_general(matrix, matrix, (((0,), (0,)), ((), ())), precision=lax.Precision.HIGHEST)

def right_solve(lower_factor, matrix):
    return lax.linalg.triangular_solve(lower_factor, matrix, left_side=False, lower=True, transpose_a=True)

def reference(slab, exponents, sketch):
    grouped_values = slab.reshape(N_TEX, TEX_DEV, DIRS)
    grouped_exponents = exponents.reshape(N_TEX, TEX_DEV // BLOCK, DIRS // BLOCK)
    mapped = lax.map(lambda operands: sketch_group(operands, sketch), (grouped_values, grouped_exponents))
    sketched = mapped.reshape(TEXELS, R)
    lower_factor = jnp.linalg.cholesky(column_gram(sketched))
    orthonormal = right_solve(lower_factor, sketched)
    return (orthonormal * math.sqrt(TEXELS)).astype(jnp.bfloat16)
```

```python
import math

import jax
import jax.numpy as jnp
from jax import lax
from jax.sharding import Mesh, PartitionSpec as P

TILE = 128
PLANE = ("dir", "y", "core")


def scales_of(exponent_table):
    total = jnp.zeros(exponent_table.shape, jnp.float32)
    for exponent_value in range(-2, 3):
        total = total + jnp.where(
            exponent_table == exponent_value, jnp.float32(2.0**exponent_value), jnp.float32(0.0)
        )
    return total.astype(jnp.bfloat16)


def dequantize(values, exponent_table):
    height, breadth = values.shape
    edge_rows = height // exponent_table.shape[0]
    edge_cols = breadth // exponent_table.shape[1]
    scale_table = scales_of(exponent_table)
    tiled = values.reshape(exponent_table.shape[0], edge_rows, exponent_table.shape[1], edge_cols)
    tiled = tiled * scale_table[:, None, :, None]
    return tiled.reshape(height, breadth)


def right_solve(lower_factor, matrix):
    return lax.linalg.triangular_solve(
        lower_factor, matrix, left_side=False, lower=True, transpose_a=True
    )


def sum_of(pieces):
    return jnp.sum(pieces.astype(jnp.float32), axis=0)


def copies(piece, count):
    return jnp.broadcast_to(piece[None], (count,) + piece.shape)


def body(slab, exponents, sketch):
    scaled_values = dequantize(slab, exponents)
    partial_values = jnp.dot(scaled_values, sketch, preferred_element_type=jnp.float32)
    dirs = lax.axis_size("dir")
    rank = sketch.shape[1]
    parts = partial_values.astype(jnp.bfloat16).reshape(dirs, -1, rank)
    sketched = sum_of(lax.all_to_all(parts, "dir", 0, 0))

    rounded = sketched.astype(jnp.bfloat16)
    tiles = rank // TILE
    rows = []
    for i in range(tiles):
        rows.append(
            lax.dot_general(
                rounded[:, i * TILE : (i + 1) * TILE],
                rounded[:, i * TILE :],
                (((0,), (0,)), ((), ())),
                preferred_element_type=jnp.float32,
            ).astype(jnp.bfloat16)
        )
    blocks = [
        rows[i][:, (j - i) * TILE : (j - i + 1) * TILE] for i in range(tiles) for j in range(i, tiles)
    ]
    planes = lax.axis_size(PLANE)
    pieces = jnp.concatenate(blocks, axis=0).reshape(planes, -1, TILE)
    mine = sum_of(lax.all_to_all(pieces, PLANE, 0, 0)).astype(jnp.bfloat16)
    mine = sum_of(lax.all_to_all(copies(mine, lax.axis_size("z")), "z", 0, 0)).astype(jnp.bfloat16)
    merged = lax.all_to_all(copies(mine, planes), PLANE, 0, 0).reshape(-1, TILE, TILE)
    merged = merged.astype(jnp.float32)

    grid = [[None] * tiles for _ in range(tiles)]
    at = 0
    for i in range(tiles):
        for j in range(i, tiles):
            grid[i][j] = merged[at]
            grid[j][i] = merged[at].T
            at += 1
    gram = jnp.block(grid)
    lower_factor = jnp.linalg.cholesky(gram, symmetrize_input=False)
    orthonormal = right_solve(lower_factor, sketched)
    texel_count = sketched.shape[0] * lax.axis_size(("dir", "z", "y", "core"))
    return (orthonormal * math.sqrt(texel_count)).astype(jnp.bfloat16)


def solution(mesh):
    fine = Mesh(mesh.devices.reshape(4, 16, 4, 2), ("dir", "z", "y", "core"))
    tex = ("z", "y", "core")
    return jax.shard_map(
        body,
        mesh=fine,
        in_specs=(P(tex, "dir"), P(tex, "dir"), P("dir", None)),
        out_specs=P(tex + ("dir",), None),
        check_vma=False,
    )
```

```python
import functools
import math

import jax
import jax.numpy as jnp
from jax import lax
from jax.experimental import pallas as pl
from jax.experimental.pallas import tpu as pltpu
from jax.sharding import Mesh, PartitionSpec as P

f32=jnp.float32; bf=jnp.bfloat16
TILE=128; PAN=8

def halves(x):
    hi=x.astype(bf)
    return hi,(x-hi.astype(f32)).astype(bf)

def product(a,b,dims):
    (ah,al),(bh,bl)=a,b
    def dot(x,y):
        return lax.dot_general(x,y,(dims,((),())),preferred_element_type=f32)
    return dot(ah,bh)+(dot(ah,bl)+dot(al,bh))

def reciprocal(d):
    r=pl.reciprocal(d,approx=True)
    return r*(2.0-d*r)

def spread_rows(x):
    return [jnp.broadcast_to(x[i:i+1,:],x.shape) for i in range(PAN)]

def factor(a_ref, u_ref, aside):
    shape=(PAN,TILE)
    sub=lax.broadcasted_iota(jnp.int32,shape,0)
    lane=lax.broadcasted_iota(jnp.int32,shape,1)
    pa=a_ref[0:PAN,0:TILE]; pm=a_ref[0:PAN,TILE:2*TILE]
    steps=TILE//PAN
    for p in range(steps):
        c0=PAN*p
        last=p==steps-1
        columns=[jnp.broadcast_to(pa[:,c0+j:c0+j+1],shape) for j in range(PAN)]
        e=[[jnp.broadcast_to(columns[j][i:i+1,:],shape) if i>=j else None for j in range(PAN)] for i in range(PAN)]
        ua=spread_rows(pa); um=spread_rows(pm)
        if not last:
            cn=[jnp.broadcast_to(jnp.sum(jnp.where(lane==c0+PAN+sub,ua[j],0.0),axis=1,keepdims=True),shape) for j in range(PAN)]
        inv=[None]*PAN
        for j in range(PAN):
            inv[j]=reciprocal(e[j][j])
            for i in range(j+1,PAN):
                l=e[i][j]*inv[j]
                for k in range(j+1,i+1):
                    e[i][k]=e[i][k]-l*e[k][j]
                ua[i]=ua[i]-l*ua[j]
                um[i]=um[i]-l*um[j]
                if not last: cn[i]=cn[i]-l*cn[j]
        outa=jnp.zeros(shape,f32); outm=jnp.zeros(shape,f32)
        for i in range(PAN):
            rs=lax.rsqrt(e[i][i])
            outa=jnp.where(sub==i,ua[i]*rs,outa)
            outm=jnp.where(sub==i,um[i]*rs,outm)
        u_ref[c0:c0+PAN,:]=outm
        if aside: aside.pop(0)()
        if not last:
            pa=a_ref[c0+PAN:c0+2*PAN,0:TILE]; pm=a_ref[c0+PAN:c0+2*PAN,TILE:2*TILE]
            for j in range(PAN):
                w=cn[j]*inv[j]
                pa=pa-w*ua[j]; pm=pm-w*um[j]
            r0=c0+2*PAN
            if r0<TILE:
                al=outa-outa.astype(bf).astype(f32); ml=outm-outm.astype(bf).astype(f32)
                lhs=jnp.concatenate([outa,outa,al],axis=0).astype(bf)
                hi=jnp.concatenate([outa,outm],axis=1)
                lo=jnp.concatenate([al,ml],axis=1)
                rhs=jnp.concatenate([hi,lo,hi],axis=0).astype(bf)
                upd=lax.dot_general(lhs,rhs,(((0,),(0,)),((),())),preferred_element_type=f32)
                a_ref[r0:TILE,:]=a_ref[r0:TILE,:]-upd[r0:TILE,:]
    while aside: aside.pop(0)()

NN=((1,),(0,)); TN=((0,),(0,)); NT=((1,),(1,))

def whiten_kernel(scale, gram_ref, s_ref, out_ref, a_ref, r_ref, f_ref, w_ref, uh_ref, ul_ref):
    rank=s_ref.shape[1]; tiles=rank//TILE
    cut=lambda i: slice(i*TILE,(i+1)*TILE)
    row=lax.broadcasted_iota(jnp.int32,(TILE,TILE),0); col=lax.broadcasted_iota(jnp.int32,(TILE,TILE),1)
    eye=jnp.where(row==col,1.0,0.0)
    at=0
    for i in range(tiles):
        for j in range(i,tiles):
            blk=gram_ref[at*TILE:(at+1)*TILE,:].astype(f32)
            if i==j==0: f_ref[:,0:TILE]=blk
            else: a_ref[cut(i),cut(j)]=blk
            at+=1
    r_ref[...]=s_ref[...].astype(f32)
    aside=[]
    for k in range(tiles):
        f_ref[:,TILE:2*TILE]=eye
        factor(f_ref,w_ref,aside)
        w=halves(w_ref[...])
        rest=slice((k+1)*TILE,rank)
        aside=[]
        if k<tiles-1:
            u=halves(product(w,halves(a_ref[cut(k),rest]),NN))
            uh_ref[cut(k),rest]=u[0]; ul_ref[cut(k),rest]=u[1]
            first=(u[0][:,0:TILE],u[1][:,0:TILE])
            f_ref[:,0:TILE]=a_ref[cut(k+1),cut(k+1)]-product(first,first,TN)
        def solve(k=k,w=w):
            q=product(halves(r_ref[:,cut(k)]),w,NT)
            out_ref[:,cut(k)]=(q*scale).astype(out_ref.dtype)
            if k<tiles-1: r_ref[:,cut(k)]=q
        def trail(i,lo,k=k):
            def run():
                a=(uh_ref[cut(k),cut(i)],ul_ref[cut(k),cut(i)])
                b=(uh_ref[cut(k),lo*TILE:rank],ul_ref[cut(k),lo*TILE:rank])
                a_ref[cut(i),lo*TILE:rank]=a_ref[cut(i),lo*TILE:rank]-product(a,b,TN)
            return run
        def carry(i,k=k):
            def run():
                u=(uh_ref[cut(k),cut(i)],ul_ref[cut(k),cut(i)])
                r_ref[:,cut(i)]=r_ref[:,cut(i)]-product(halves(r_ref[:,cut(k)]),u,NN)
            return run
        if k<tiles-1:
            if k+2<tiles: aside.append(trail(k+1,k+2))
            for i in range(k+2,tiles): aside.append(trail(i,i))
            aside.append(solve)
            for i in range(k+1,tiles): aside.append(carry(i))
        else: solve()

def whiten(gram,s,scale):
    rows,rank=s.shape
    return pl.pallas_call(functools.partial(whiten_kernel,scale),out_shape=jax.ShapeDtypeStruct((rows,rank),bf),
        scratch_shapes=[pltpu.VMEM((rank,rank),f32),pltpu.VMEM((rows,rank),f32),pltpu.VMEM((TILE,2*TILE),f32),pltpu.VMEM((TILE,TILE),f32),pltpu.VMEM((rank,rank),bf),pltpu.VMEM((rank,rank),bf)],
        compiler_params=pltpu.CompilerParams(vmem_limit_bytes=32*1024*1024),)(gram,s)

PLANE = ("dir", "y", "core")


def scales_of(exponent_table):
    total = jnp.zeros(exponent_table.shape, jnp.float32)
    for exponent_value in range(-2, 3):
        total = total + jnp.where(
            exponent_table == exponent_value, jnp.float32(2.0**exponent_value), jnp.float32(0.0)
        )
    return total.astype(jnp.bfloat16)


def dequantize(values, exponent_table):
    height, breadth = values.shape
    edge_rows = height // exponent_table.shape[0]
    edge_cols = breadth // exponent_table.shape[1]
    scale_table = scales_of(exponent_table)
    tiled = values.reshape(exponent_table.shape[0], edge_rows, exponent_table.shape[1], edge_cols)
    tiled = tiled * scale_table[:, None, :, None]
    return tiled.reshape(height, breadth)


def sum_of(pieces):
    return jnp.sum(pieces.astype(jnp.float32), axis=0)


def copies(piece, count):
    return jnp.broadcast_to(piece[None], (count,) + piece.shape)


def body(slab, exponents, sketch):
    scaled_values = dequantize(slab, exponents)
    partial_values = jnp.dot(scaled_values, sketch, preferred_element_type=jnp.float32)
    dirs = lax.axis_size("dir")
    rank = sketch.shape[1]
    parts = partial_values.astype(jnp.bfloat16).reshape(dirs, -1, rank)
    sketched = sum_of(lax.all_to_all(parts, "dir", 0, 0))

    rounded = sketched.astype(jnp.bfloat16)
    tiles = rank // TILE
    rows = []
    for i in range(tiles):
        rows.append(
            lax.dot_general(
                rounded[:, i * TILE : (i + 1) * TILE],
                rounded[:, i * TILE :],
                (((0,), (0,)), ((), ())),
                preferred_element_type=jnp.float32,
            ).astype(jnp.bfloat16)
        )
    blocks = [
        rows[i][:, (j - i) * TILE : (j - i + 1) * TILE] for i in range(tiles) for j in range(i, tiles)
    ]
    planes = lax.axis_size(PLANE)
    pieces = jnp.concatenate(blocks, axis=0).reshape(planes, -1, TILE)
    mine = sum_of(lax.all_to_all(pieces, PLANE, 0, 0)).astype(jnp.bfloat16)
    mine = sum_of(lax.all_to_all(copies(mine, lax.axis_size("z")), "z", 0, 0)).astype(jnp.bfloat16)
    merged = lax.all_to_all(copies(mine, planes), PLANE, 0, 0).reshape(-1, TILE)
    texel_count = sketched.shape[0] * lax.axis_size(("dir", "z", "y", "core"))
    return whiten(merged, rounded, math.sqrt(texel_count))


def solution(mesh):
    fine = Mesh(mesh.devices.reshape(4, 16, 4, 2), ("dir", "z", "y", "core"))
    tex = ("z", "y", "core")
    return jax.shard_map(
        body,
        mesh=fine,
        in_specs=(P(tex, "dir"), P(tex, "dir"), P("dir", None)),
        out_specs=P(tex + ("dir",), None),
        check_vma=False,
    )
```

```python
import functools
import math

import jax
import jax.numpy as jnp
import numpy as np
from jax import lax
from jax.experimental import pallas as pl
from jax.experimental.pallas import tpu as pltpu
from jax.sharding import Mesh, PartitionSpec as P

f32 = jnp.float32
bf16 = jnp.bfloat16
TILE = 128
PANEL = 8
NN = ((1,), (0,))
TN = ((0,), (0,))
NT = ((1,), (1,))


def cut(i):
    return slice(i * TILE, (i + 1) * TILE)


def halves(x):
    high = x.astype(bf16)
    return high, (x - high.astype(f32)).astype(bf16)


def product(a, b, dims):
    def dot(x, y):
        return lax.dot_general(x, y, (dims, ((), ())), preferred_element_type=f32)

    return dot(a[0], b[0]) + (dot(a[0], b[1]) + dot(a[1], b[0]))


def places():
    shape = (TILE, TILE)
    return lax.broadcasted_iota(jnp.int32, shape, 0), lax.broadcasted_iota(jnp.int32, shape, 1)


def tree(terms):
    while len(terms) > 1:
        odd = terms[len(terms) // 2 * 2 :]
        terms = [terms[i] + terms[i + 1] for i in range(0, len(terms) - 1, 2)] + odd
    return terms[0]


def factor(a_ref, w_ref, t_ref, aside):
    shape = (PANEL, TILE)
    sub = lax.broadcasted_iota(jnp.int32, shape, 0)
    lane = lax.broadcasted_iota(jnp.int32, shape, 1)
    steps = TILE // PANEL
    pa, pm = a_ref[0:PANEL, 0:TILE], a_ref[0:PANEL, TILE : 2 * TILE]
    for p in range(steps):
        at, after = p * PANEL, (p + 1) * PANEL
        base = p % 2 * PANEL * PANEL
        for j in range(PANEL):
            spread = jnp.broadcast_to(pa[:, at + j : at + j + 1], shape)
            t_ref[base + PANEL * j : base + PANEL * (j + 1), :] = spread
        e = [
            [t_ref[pl.ds(base + PANEL * j + i, PANEL, stride=0), :] for j in range(i + 1)]
            for i in range(PANEL)
        ]
        ua = [jnp.broadcast_to(pa[i : i + 1, :], shape) for i in range(PANEL)]
        um = [jnp.broadcast_to(pm[i : i + 1, :], shape) for i in range(PANEL)]
        more = p < steps - 1
        if more:
            here = lane == after + sub
            nxt = [
                jnp.broadcast_to(
                    jnp.sum(jnp.where(here, ua[j], 0.0), axis=1, keepdims=True), shape
                )
                for j in range(PANEL)
            ]
        inv = []
        for j in range(PANEL):
            inv.append(pl.reciprocal(e[j][j], approx=True))
            for i in range(j + 1, PANEL):
                ratio = e[i][j] * inv[j]
                for k in range(j + 1, i + 1):
                    e[i][k] = e[i][k] - ratio * e[k][j]
                ua[i] = ua[i] - ratio * ua[j]
                um[i] = um[i] - ratio * um[j]
                if more:
                    nxt[i] = nxt[i] - ratio * nxt[j]
        if more:
            weights = [nxt[j] * inv[j] for j in range(PANEL)]
            rows = slice(after, after + PANEL)
            pa = a_ref[rows, 0:TILE] - tree([w * u for w, u in zip(weights, ua)])
            pm = a_ref[rows, TILE : 2 * TILE] - tree([w * u for w, u in zip(weights, um)])
        outa, outm, pivots = ua[0], um[0], e[0][0]
        for i in range(1, PANEL):
            outa = jnp.where(sub == i, ua[i], outa)
            outm = jnp.where(sub == i, um[i], outm)
            pivots = jnp.where(sub == i, e[i][i], pivots)
        root = lax.rsqrt(pivots)
        outa, outm = outa * root, outm * root
        w_ref[at:after, :] = outm
        if aside:
            aside.pop(0)()
        rest = after + PANEL
        if rest < TILE:
            lowa = outa - outa.astype(bf16).astype(f32)
            lowm = outm - outm.astype(bf16).astype(f32)
            none = jnp.zeros(shape, f32)
            high = jnp.concatenate([outa, outm], axis=1)
            low = jnp.concatenate([lowa, lowm], axis=1)
            left = jnp.concatenate([outa, outa, lowa, none], axis=0).astype(bf16)
            right = jnp.concatenate([high, low, high, jnp.zeros_like(low)], axis=0).astype(bf16)
            update = lax.dot_general(left, right, (TN, ((), ())), preferred_element_type=f32)
            a_ref[rest:TILE, :] = a_ref[rest:TILE, :] - update[rest:TILE, :]
    while aside:
        aside.pop(0)()


def gram_kernel(parts_ref, s_ref, gram_ref):
    total = parts_ref[0].astype(f32)
    for g in range(1, parts_ref.shape[0]):
        total = total + parts_ref[g].astype(f32)
    s_ref[...] = total.astype(bf16)
    rank = s_ref.shape[1]
    tiles = rank // TILE
    row, col = places()
    at = tiles // 2
    diagonal = []
    for i in range(tiles):
        strip = lax.dot_general(
            s_ref[:, cut(i)],
            s_ref[:, i * TILE : rank],
            (TN, ((), ())),
            preferred_element_type=f32,
        )
        diagonal.append(strip[:, 0:TILE])
        for j in range(1, tiles - i):
            gram_ref[cut(at), :] = strip[:, cut(j)].astype(bf16)
            at += 1
    tail = []
    for i in range(0, tiles, 2):
        gram_ref[cut(i // 2), :] = jnp.where(col >= row, diagonal[i], diagonal[i + 1]).astype(bf16)
        tail.append(jnp.sum(jnp.where(row == col, diagonal[i + 1], 0.0), axis=0, keepdims=True))
    rest = gram_ref.shape[0] - at * TILE
    tail.append(jnp.zeros((rest - len(tail), TILE), f32))
    gram_ref[at * TILE : at * TILE + rest, :] = jnp.concatenate(tail, axis=0).astype(bf16)


def local_gram(parts, height):
    rows, rank = parts.shape[1:]
    return pl.pallas_call(
        gram_kernel,
        out_shape=(
            jax.ShapeDtypeStruct((rows, rank), bf16),
            jax.ShapeDtypeStruct((height, TILE), bf16),
        ),
        compiler_params=pltpu.CompilerParams(vmem_limit_bytes=32 * 1024 * 1024),
    )(parts)


def whiten_kernel(scale, gram_ref, s_ref, out_ref, a_ref, r_ref, f_ref, w_ref, t_ref, uh_ref, ul_ref):
    rank = s_ref.shape[1]
    tiles = rank // TILE
    row, col = places()
    eye = jnp.where(row == col, 1.0, 0.0)
    at = tiles // 2
    offset = tiles // 2 * TILE + tiles * (tiles - 1) // 2 * TILE
    tail = gram_ref[offset : offset + 16, :].astype(f32)
    for i in range(0, tiles, 2):
        pair = gram_ref[cut(i // 2), :].astype(f32)
        turned = jnp.transpose(pair)
        first = jnp.where(col >= row, pair, turned)
        second = jnp.where(col < row, pair, turned)
        second = jnp.where(row == col, tail[i // 2 : i // 2 + 1, :], second)
        if i == 0:
            f_ref[:, 0:TILE] = first
        else:
            a_ref[cut(i), cut(i)] = first
        a_ref[cut(i + 1), cut(i + 1)] = second
    for i in range(tiles):
        for j in range(i + 1, tiles):
            a_ref[cut(i), cut(j)] = gram_ref[cut(at), :].astype(f32)
            at += 1
    r_ref[...] = s_ref[...].astype(f32)
    aside = []
    for k in range(tiles):
        f_ref[:, TILE : 2 * TILE] = eye
        factor(f_ref, w_ref, t_ref, aside)
        w = halves(w_ref[...])
        aside = []
        last = k == tiles - 1
        if not last:
            rest = slice((k + 1) * TILE, rank)
            u = halves(product(w, halves(a_ref[cut(k), rest]), NN))
            uh_ref[cut(k), rest], ul_ref[cut(k), rest] = u
            near = (u[0][:, 0:TILE], u[1][:, 0:TILE])
            f_ref[:, 0:TILE] = a_ref[cut(k + 1), cut(k + 1)] - product(near, near, TN)

        def solve(k=k, w=w, last=last):
            q = product(halves(r_ref[:, cut(k)]), w, NT)
            out_ref[:, cut(k)] = (q * scale).astype(out_ref.dtype)
            if not last:
                r_ref[:, cut(k)] = q

        def trail(i, low, k=k):
            wide = slice(low * TILE, rank)
            a = (uh_ref[cut(k), cut(i)], ul_ref[cut(k), cut(i)])
            b = (uh_ref[cut(k), wide], ul_ref[cut(k), wide])
            a_ref[cut(i), wide] = a_ref[cut(i), wide] - product(a, b, TN)

        def carry(i, k=k):
            u = (uh_ref[cut(k), cut(i)], ul_ref[cut(k), cut(i)])
            r_ref[:, cut(i)] = r_ref[:, cut(i)] - product(halves(r_ref[:, cut(k)]), u, NN)

        if last:
            solve()
        else:
            if k + 2 < tiles:
                aside.append(functools.partial(trail, k + 1, k + 2))
            for i in range(k + 2, tiles):
                aside.append(functools.partial(trail, i, i))
            aside.append(solve)
            for i in range(k + 1, tiles):
                aside.append(functools.partial(carry, i))


def whiten(gram, s, scale):
    rows, rank = s.shape
    return pl.pallas_call(
        functools.partial(whiten_kernel, scale),
        out_shape=jax.ShapeDtypeStruct((rows, rank), bf16),
        scratch_shapes=[
            pltpu.VMEM((rank, rank), f32),
            pltpu.VMEM((rows, rank), f32),
            pltpu.VMEM((TILE, 2 * TILE), f32),
            pltpu.VMEM((TILE, TILE), f32),
            pltpu.VMEM((2 * PANEL * PANEL, TILE), f32),
            pltpu.VMEM((rank, rank), bf16),
            pltpu.VMEM((rank, rank), bf16),
        ],
        compiler_params=pltpu.CompilerParams(vmem_limit_bytes=32 * 1024 * 1024),
    )(gram, s)


PLANE = ("dir", "y", "core")


def scales_of(exponent_table):
    total = jnp.zeros(exponent_table.shape, jnp.float32)
    for exponent_value in range(-2, 3):
        total = total + jnp.where(
            exponent_table == exponent_value, jnp.float32(2.0**exponent_value), jnp.float32(0.0)
        )
    return total.astype(jnp.bfloat16)


def dequantize(values, exponent_table):
    height, breadth = values.shape
    edge_rows = height // exponent_table.shape[0]
    edge_cols = breadth // exponent_table.shape[1]
    scale_table = scales_of(exponent_table)
    tiled = values.reshape(exponent_table.shape[0], edge_rows, exponent_table.shape[1], edge_cols)
    tiled = tiled * scale_table[:, None, :, None]
    return tiled.reshape(height, breadth)


def exchange(pieces, count, axes):
    shape = pieces.shape
    paired = pieces.reshape(count, -1, 2, TILE)
    return lax.all_to_all(paired, axes, 0, 0).reshape(shape)


def sum_and_copy(pieces, count, copies):
    size = pieces.shape[0] // count
    chooser = jnp.asarray(np.tile(np.eye(size), (copies, count)), jnp.bfloat16)
    return jnp.dot(chooser, pieces, preferred_element_type=jnp.float32).astype(jnp.bfloat16)


def body(slab, exponents, sketch):
    scaled_values = dequantize(slab, exponents)
    partial_values = jnp.dot(scaled_values, sketch, preferred_element_type=jnp.float32)
    dirs, planes, depth = (lax.axis_size(axes) for axes in ("dir", PLANE, "z"))
    rank = sketch.shape[1]
    parts = partial_values.astype(jnp.bfloat16).reshape(dirs, -1, rank)
    parts = lax.all_to_all(parts, "dir", 0, 0)

    tiles = rank // TILE
    distinct = tiles * tiles // 2 * TILE + tiles // 2
    height = -(-distinct // (2 * planes)) * 2 * planes
    sketched, gram = local_gram(parts, height)
    gram = exchange(gram, planes, PLANE)
    gram = exchange(sum_and_copy(gram, planes, depth), depth, "z")
    gram = exchange(sum_and_copy(gram, depth, planes), planes, PLANE)
    texel_count = sketched.shape[0] * planes * depth
    return whiten(gram, sketched, math.sqrt(texel_count))


def solution(mesh):
    fine = Mesh(mesh.devices.reshape(4, 16, 4, 2), ("dir", "z", "y", "core"))
    tex = ("z", "y", "core")
    return jax.shard_map(
        body,
        mesh=fine,
        in_specs=(P(tex, "dir"), P(tex, "dir"), P("dir", None)),
        out_specs=P(tex + ("dir",), None),
        check_vma=False,
    )
```

```python
import functools
import math

import jax
import jax.numpy as jnp
import numpy as np
from jax import lax
from jax.experimental import pallas as pl
from jax.experimental.pallas import tpu as pltpu
from jax.sharding import Mesh, PartitionSpec as P

f32 = jnp.float32
bf16 = jnp.bfloat16
TILE = 128
PANEL = 8
NN = ((1,), (0,))
TN = ((0,), (0,))
NT = ((1,), (1,))


def cut(i):
    return slice(i * TILE, (i + 1) * TILE)


def halves(x):
    high = x.astype(bf16)
    return high, (x - high.astype(f32)).astype(bf16)


def product(a, b, dims):
    def dot(x, y):
        return lax.dot_general(x, y, (dims, ((), ())), preferred_element_type=f32)

    return dot(a[0], b[0]) + (dot(a[0], b[1]) + dot(a[1], b[0]))


def places():
    shape = (TILE, TILE)
    return lax.broadcasted_iota(jnp.int32, shape, 0), lax.broadcasted_iota(jnp.int32, shape, 1)


def tree(terms):
    while len(terms) > 1:
        odd = terms[len(terms) // 2 * 2 :]
        terms = [terms[i] + terms[i + 1] for i in range(0, len(terms) - 1, 2)] + odd
    return terms[0]


def factor(a_ref, w_ref, t_ref, aside):
    shape = (PANEL, TILE)
    sub = lax.broadcasted_iota(jnp.int32, shape, 0)
    lane = lax.broadcasted_iota(jnp.int32, shape, 1)
    steps = TILE // PANEL
    pa, pm = a_ref[0:PANEL, 0:TILE], a_ref[0:PANEL, TILE : 2 * TILE]
    for p in range(steps):
        at, after = p * PANEL, (p + 1) * PANEL
        base = p % 2 * PANEL * PANEL
        for j in range(PANEL):
            spread = jnp.broadcast_to(pa[:, at + j : at + j + 1], shape)
            t_ref[base + PANEL * j : base + PANEL * (j + 1), :] = spread
        e = [
            [t_ref[pl.ds(base + PANEL * j + i, PANEL, stride=0), :] for j in range(i + 1)]
            for i in range(PANEL)
        ]
        ua = [jnp.broadcast_to(pa[i : i + 1, :], shape) for i in range(PANEL)]
        um = [jnp.broadcast_to(pm[i : i + 1, :], shape) for i in range(PANEL)]
        more = p < steps - 1
        if more:
            here = lane == after + sub
            nxt = [
                jnp.broadcast_to(
                    jnp.sum(jnp.where(here, ua[j], 0.0), axis=1, keepdims=True), shape
                )
                for j in range(PANEL)
            ]
        inv = []
        for j in range(PANEL):
            inv.append(pl.reciprocal(e[j][j], approx=True))
            for i in range(j + 1, PANEL):
                ratio = e[i][j] * inv[j]
                for k in range(j + 1, i + 1):
                    e[i][k] = e[i][k] - ratio * e[k][j]
                ua[i] = ua[i] - ratio * ua[j]
                um[i] = um[i] - ratio * um[j]
                if more:
                    nxt[i] = nxt[i] - ratio * nxt[j]
        if more:
            weights = [nxt[j] * inv[j] for j in range(PANEL)]
            rows = slice(after, after + PANEL)
            pa = a_ref[rows, 0:TILE] - tree([w * u for w, u in zip(weights, ua)])
            pm = a_ref[rows, TILE : 2 * TILE] - tree([w * u for w, u in zip(weights, um)])
        outa, outm, pivots = ua[0], um[0], e[0][0]
        for i in range(1, PANEL):
            outa = jnp.where(sub == i, ua[i], outa)
            outm = jnp.where(sub == i, um[i], outm)
            pivots = jnp.where(sub == i, e[i][i], pivots)
        root = lax.rsqrt(pivots)
        outa, outm = outa * root, outm * root
        w_ref[at:after, :] = outm
        if aside:
            aside.pop(0)()
        rest = after + PANEL
        if rest < TILE:
            lowa = outa - outa.astype(bf16).astype(f32)
            lowm = outm - outm.astype(bf16).astype(f32)
            none = jnp.zeros(shape, f32)
            high = jnp.concatenate([outa, outm], axis=1)
            low = jnp.concatenate([lowa, lowm], axis=1)
            left = jnp.concatenate([outa, outa, lowa, none], axis=0).astype(bf16)
            right = jnp.concatenate([high, low, high, jnp.zeros_like(low)], axis=0).astype(bf16)
            update = lax.dot_general(left, right, (TN, ((), ())), preferred_element_type=f32)
            a_ref[rest:TILE, :] = a_ref[rest:TILE, :] - update[rest:TILE, :]
    while aside:
        aside.pop(0)()


def gram_kernel(parts_ref, s_ref, gram_ref):
    total = parts_ref[0].astype(f32)
    for g in range(1, parts_ref.shape[0]):
        total = total + parts_ref[g].astype(f32)
    s_ref[...] = total.astype(bf16)
    rank = s_ref.shape[1]
    tiles = rank // TILE
    row, col = places()
    at = tiles // 2
    diagonal = []
    for i in range(tiles):
        strip = lax.dot_general(
            s_ref[:, cut(i)],
            s_ref[:, i * TILE : rank],
            (TN, ((), ())),
            preferred_element_type=f32,
        )
        diagonal.append(strip[:, 0:TILE])
        for j in range(1, tiles - i):
            gram_ref[cut(at), :] = strip[:, cut(j)].astype(bf16)
            at += 1
    tail = []
    for i in range(0, tiles, 2):
        gram_ref[cut(i // 2), :] = jnp.where(col >= row, diagonal[i], diagonal[i + 1]).astype(bf16)
        tail.append(jnp.sum(jnp.where(row == col, diagonal[i + 1], 0.0), axis=0, keepdims=True))
    rest = gram_ref.shape[0] - at * TILE
    tail.append(jnp.zeros((rest - len(tail), TILE), f32))
    gram_ref[at * TILE : at * TILE + rest, :] = jnp.concatenate(tail, axis=0).astype(bf16)


def local_gram(parts, height):
    rows, rank = parts.shape[1:]
    return pl.pallas_call(
        gram_kernel,
        out_shape=(
            jax.ShapeDtypeStruct((rows, rank), bf16),
            jax.ShapeDtypeStruct((height, TILE), bf16),
        ),
        compiler_params=pltpu.CompilerParams(vmem_limit_bytes=32 * 1024 * 1024),
    )(parts)


def whiten_kernel(scale, gram_ref, s_ref, out_ref, a_ref, r_ref, f_ref, w_ref, t_ref, uh_ref, ul_ref):
    rank = s_ref.shape[1]
    tiles = rank // TILE
    row, col = places()
    eye = jnp.where(row == col, 1.0, 0.0)
    across = tiles // 2
    offset = (across + tiles * (tiles - 1) // 2) * TILE

    def unpack(i):
        pair = gram_ref[cut(i // 2), :].astype(f32)
        turned = jnp.transpose(pair)
        tail = gram_ref[offset : offset + 16, :].astype(f32)
        second = jnp.where(col < row, pair, turned)
        second = jnp.where(row == col, tail[i // 2 : i // 2 + 1, :], second)
        if i > 0:
            a_ref[cut(i), cut(i)] = jnp.where(col >= row, pair, turned)
        a_ref[cut(i + 1), cut(i + 1)] = second

    def widen(i):
        start = across + i * (tiles - 1) - i * (i - 1) // 2
        for j in range(i + 1, tiles):
            a_ref[cut(i), cut(j)] = gram_ref[cut(start + j - i - 1), :].astype(f32)

    pair = gram_ref[cut(0), :].astype(f32)
    f_ref[:, 0:TILE] = jnp.where(col >= row, pair, jnp.transpose(pair))
    aside = [functools.partial(unpack, i) for i in range(0, tiles, 2)]
    aside += [functools.partial(widen, i) for i in range(tiles - 1)]
    for k in range(tiles):
        f_ref[:, TILE : 2 * TILE] = eye
        factor(f_ref, w_ref, t_ref, aside)
        w = halves(w_ref[...])
        aside = []
        last = k == tiles - 1
        if not last:
            row_k = halves(a_ref[cut(k), (k + 1) * TILE : rank])
            near = halves(product(w, (row_k[0][:, 0:TILE], row_k[1][:, 0:TILE]), NN))
            f_ref[:, 0:TILE] = a_ref[cut(k + 1), cut(k + 1)] - product(near, near, TN)
            uh_ref[cut(k), cut(k + 1)], ul_ref[cut(k), cut(k + 1)] = near

        def spread(k=k, w=w):
            wide = slice((k + 2) * TILE, rank)
            uh_ref[cut(k), wide], ul_ref[cut(k), wide] = halves(
                product(w, halves(a_ref[cut(k), wide]), NN)
            )

        def solve(k=k, w=w, last=last):
            own = s_ref[:, cut(k)] if k == 0 else r_ref[:, cut(k)]
            if k == 0:
                q = lax.dot_general(own, w[0], (NT, ((), ())), preferred_element_type=f32)
                q = q + lax.dot_general(own, w[1], (NT, ((), ())), preferred_element_type=f32)
            else:
                q = product(halves(own), w, NT)
            out_ref[:, cut(k)] = (q * scale).astype(out_ref.dtype)
            if not last:
                r_ref[:, cut(k)] = q

        def trail(i, low, k=k):
            wide = slice(low * TILE, rank)
            a = (uh_ref[cut(k), cut(i)], ul_ref[cut(k), cut(i)])
            b = (uh_ref[cut(k), wide], ul_ref[cut(k), wide])
            a_ref[cut(i), wide] = a_ref[cut(i), wide] - product(a, b, TN)

        def carry(i, k=k):
            u = (uh_ref[cut(k), cut(i)], ul_ref[cut(k), cut(i)])
            own = s_ref[:, cut(i)].astype(f32) if k == 0 else r_ref[:, cut(i)]
            r_ref[:, cut(i)] = own - product(halves(r_ref[:, cut(k)]), u, NN)

        if last:
            solve()
        else:
            if k + 2 < tiles:
                aside.append(spread)
                aside.append(functools.partial(trail, k + 1, k + 2))
            for i in range(k + 2, tiles):
                aside.append(functools.partial(trail, i, i))
            aside.append(solve)
            for i in range(k + 1, tiles):
                aside.append(functools.partial(carry, i))


def whiten(gram, s, scale):
    rows, rank = s.shape
    return pl.pallas_call(
        functools.partial(whiten_kernel, scale),
        out_shape=jax.ShapeDtypeStruct((rows, rank), bf16),
        scratch_shapes=[
            pltpu.VMEM((rank, rank), f32),
            pltpu.VMEM((rows, rank), f32),
            pltpu.VMEM((TILE, 2 * TILE), f32),
            pltpu.VMEM((TILE, TILE), f32),
            pltpu.VMEM((2 * PANEL * PANEL, TILE), f32),
            pltpu.VMEM((rank, rank), bf16),
            pltpu.VMEM((rank, rank), bf16),
        ],
        compiler_params=pltpu.CompilerParams(vmem_limit_bytes=32 * 1024 * 1024),
    )(gram, s)


PLANE = ("dir", "y", "core")


def scales_of(exponent_table):
    total = jnp.zeros(exponent_table.shape, jnp.float32)
    for exponent_value in range(-2, 3):
        total = total + jnp.where(
            exponent_table == exponent_value, jnp.float32(2.0**exponent_value), jnp.float32(0.0)
        )
    return total.astype(jnp.bfloat16)


def dequantize(values, exponent_table):
    height, breadth = values.shape
    edge_rows = height // exponent_table.shape[0]
    edge_cols = breadth // exponent_table.shape[1]
    scale_table = scales_of(exponent_table)
    tiled = values.reshape(exponent_table.shape[0], edge_rows, exponent_table.shape[1], edge_cols)
    tiled = tiled * scale_table[:, None, :, None]
    return tiled.reshape(height, breadth)


def exchange(pieces, count, axes, order=None):
    shape = pieces.shape
    paired = pieces.reshape(count, -1, 2, TILE)
    groups = None if order is None else [order]
    return lax.all_to_all(paired, axes, 0, 0, axis_index_groups=groups).reshape(shape)


def sum_and_copy(pieces, count, copies):
    size = pieces.shape[0] // count
    chooser = jnp.asarray(np.tile(np.eye(size), (copies, count)), jnp.bfloat16)
    return jnp.dot(chooser, pieces, preferred_element_type=jnp.float32).astype(jnp.bfloat16)


def body(slab, exponents, sketch):
    scaled_values = dequantize(slab, exponents)
    partial_values = jnp.dot(scaled_values, sketch, preferred_element_type=jnp.float32)
    dirs, planes, depth = (lax.axis_size(axes) for axes in ("dir", PLANE, "z"))
    rank = sketch.shape[1]
    parts = partial_values.astype(jnp.bfloat16).reshape(dirs, -1, rank)
    parts = lax.all_to_all(parts, "dir", 0, 0)

    tiles = rank // TILE
    distinct = tiles * tiles // 2 * TILE + tiles // 2
    height = -(-distinct // (2 * planes)) * 2 * planes
    sketched, gram = local_gram(parts, height)
    gram = exchange(gram, planes, PLANE)
    order = [(z + depth // 2) % depth for z in range(depth)]
    gram = exchange(sum_and_copy(gram, planes, depth), depth, "z", order)
    gram = exchange(sum_and_copy(gram, depth, planes), planes, PLANE)
    texel_count = sketched.shape[0] * planes * depth
    return whiten(gram, sketched, math.sqrt(texel_count))


def solution(mesh):
    fine = Mesh(mesh.devices.reshape(4, 16, 4, 2), ("dir", "z", "y", "core"))
    tex = ("z", "y", "core")
    return jax.shard_map(
        body,
        mesh=fine,
        in_specs=(P(tex, "dir"), P(tex, "dir"), P("dir", None)),
        out_specs=P(tex + ("dir",), None),
        check_vma=False,
    )
```

```python
import functools
import math

import jax
import jax.numpy as jnp
import numpy as np
from jax import lax
from jax.experimental import pallas as pl
from jax.experimental.pallas import tpu as pltpu
from jax.sharding import Mesh, PartitionSpec as P

f32 = jnp.float32
bf16 = jnp.bfloat16
TILE = 128
PANEL = 8
NN = ((1,), (0,))
TN = ((0,), (0,))
NT = ((1,), (1,))


def cut(i):
    return slice(i * TILE, (i + 1) * TILE)


def halves(x):
    high = x.astype(bf16)
    return high, (x - high.astype(f32)).astype(bf16)


def product(a, b, dims):
    def dot(x, y):
        return lax.dot_general(x, y, (dims, ((), ())), preferred_element_type=f32)

    return dot(a[0], b[0]) + (dot(a[0], b[1]) + dot(a[1], b[0]))


def places():
    shape = (TILE, TILE)
    return lax.broadcasted_iota(jnp.int32, shape, 0), lax.broadcasted_iota(jnp.int32, shape, 1)


def tree(terms):
    while len(terms) > 1:
        odd = terms[len(terms) // 2 * 2 :]
        terms = [terms[i] + terms[i + 1] for i in range(0, len(terms) - 1, 2)] + odd
    return terms[0]


def factor(a_ref, w_ref, t_ref, aside):
    shape = (PANEL, TILE)
    sub = lax.broadcasted_iota(jnp.int32, shape, 0)
    lane = lax.broadcasted_iota(jnp.int32, shape, 1)
    steps = TILE // PANEL
    pa, pm = a_ref[0:PANEL, 0:TILE], a_ref[0:PANEL, TILE : 2 * TILE]
    for p in range(steps):
        at, after = p * PANEL, (p + 1) * PANEL
        base = p % 2 * PANEL * PANEL
        for j in range(PANEL):
            spread = jnp.broadcast_to(pa[:, at + j : at + j + 1], shape)
            t_ref[base + PANEL * j : base + PANEL * (j + 1), :] = spread
        e = [
            [t_ref[pl.ds(base + PANEL * j + i, PANEL, stride=0), :] for j in range(i + 1)]
            for i in range(PANEL)
        ]
        ua = [jnp.broadcast_to(pa[i : i + 1, :], shape) for i in range(PANEL)]
        um = [jnp.broadcast_to(pm[i : i + 1, :], shape) for i in range(PANEL)]
        more = p < steps - 1
        if more:
            here = lane == after + sub
            nxt = [
                jnp.broadcast_to(
                    jnp.sum(jnp.where(here, ua[j], 0.0), axis=1, keepdims=True), shape
                )
                for j in range(PANEL)
            ]
        inv = []
        for j in range(PANEL):
            inv.append(pl.reciprocal(e[j][j], approx=True))
            for i in range(j + 1, PANEL):
                ratio = e[i][j] * inv[j]
                for k in range(j + 1, i + 1):
                    e[i][k] = e[i][k] - ratio * e[k][j]
                ua[i] = ua[i] - ratio * ua[j]
                um[i] = um[i] - ratio * um[j]
                if more:
                    nxt[i] = nxt[i] - ratio * nxt[j]
        if more:
            weights = [nxt[j] * inv[j] for j in range(PANEL)]
            rows = slice(after, after + PANEL)
            pa = a_ref[rows, 0:TILE] - tree([w * u for w, u in zip(weights, ua)])
            pm = a_ref[rows, TILE : 2 * TILE] - tree([w * u for w, u in zip(weights, um)])
        outa, outm, pivots = ua[0], um[0], e[0][0]
        for i in range(1, PANEL):
            outa = jnp.where(sub == i, ua[i], outa)
            outm = jnp.where(sub == i, um[i], outm)
            pivots = jnp.where(sub == i, e[i][i], pivots)
        root = lax.rsqrt(pivots)
        outa, outm = outa * root, outm * root
        w_ref[at:after, :] = outm
        if aside:
            aside.pop(0)()
        rest = after + PANEL
        if rest < TILE:
            lowa = outa - outa.astype(bf16).astype(f32)
            lowm = outm - outm.astype(bf16).astype(f32)
            none = jnp.zeros(shape, f32)
            high = jnp.concatenate([outa, outm], axis=1)
            low = jnp.concatenate([lowa, lowm], axis=1)
            left = jnp.concatenate([outa, outa, lowa, none], axis=0).astype(bf16)
            right = jnp.concatenate([high, low, high, jnp.zeros_like(low)], axis=0).astype(bf16)
            update = lax.dot_general(left, right, (TN, ((), ())), preferred_element_type=f32)
            a_ref[rest:TILE, :] = a_ref[rest:TILE, :] - update[rest:TILE, :]
    while aside:
        aside.pop(0)()


def gram_kernel(parts_ref, s_ref, gram_ref):
    total = parts_ref[0].astype(f32)
    for g in range(1, parts_ref.shape[0]):
        total = total + parts_ref[g].astype(f32)
    s_ref[...] = total.astype(bf16)
    rank = s_ref.shape[1]
    tiles = rank // TILE
    row, col = places()
    at = tiles // 2
    diagonal = []
    for i in range(tiles):
        strip = lax.dot_general(
            s_ref[:, cut(i)],
            s_ref[:, i * TILE : rank],
            (TN, ((), ())),
            preferred_element_type=f32,
        )
        diagonal.append(strip[:, 0:TILE])
        for j in range(1, tiles - i):
            gram_ref[cut(at), :] = strip[:, cut(j)].astype(bf16)
            at += 1
    tail = []
    for i in range(0, tiles, 2):
        gram_ref[cut(i // 2), :] = jnp.where(col >= row, diagonal[i], diagonal[i + 1]).astype(bf16)
        tail.append(jnp.sum(jnp.where(row == col, diagonal[i + 1], 0.0), axis=0, keepdims=True))
    rest = gram_ref.shape[0] - at * TILE
    tail.append(jnp.zeros((rest - len(tail), TILE), f32))
    gram_ref[at * TILE : at * TILE + rest, :] = jnp.concatenate(tail, axis=0).astype(bf16)


def local_gram(parts, height):
    rows, rank = parts.shape[1:]
    return pl.pallas_call(
        gram_kernel,
        out_shape=(
            jax.ShapeDtypeStruct((rows, rank), bf16),
            jax.ShapeDtypeStruct((height, TILE), bf16),
        ),
        compiler_params=pltpu.CompilerParams(vmem_limit_bytes=32 * 1024 * 1024),
    )(parts)


def whiten_kernel(scale, gram_ref, s_ref, out_ref, a_ref, r_ref, f_ref, w_ref, t_ref, uh_ref, ul_ref):
    rank = s_ref.shape[1]
    tiles = rank // TILE
    row, col = places()
    eye = jnp.where(row == col, 1.0, 0.0)
    across = tiles // 2
    offset = (across + tiles * (tiles - 1) // 2) * TILE

    def unpack(i):
        pair = gram_ref[cut(i // 2), :].astype(f32)
        turned = jnp.transpose(pair)
        tail = gram_ref[offset : offset + 16, :].astype(f32)
        second = jnp.where(col < row, pair, turned)
        second = jnp.where(row == col, tail[i // 2 : i // 2 + 1, :], second)
        if i > 0:
            a_ref[cut(i), cut(i)] = jnp.where(col >= row, pair, turned)
        a_ref[cut(i + 1), cut(i + 1)] = second

    def widen(i):
        start = across + i * (tiles - 1) - i * (i - 1) // 2
        for j in range(i + 1, tiles):
            a_ref[cut(i), cut(j)] = gram_ref[cut(start + j - i - 1), :].astype(f32)

    pair = gram_ref[cut(0), :].astype(f32)
    f_ref[:, 0:TILE] = jnp.where(col >= row, pair, jnp.transpose(pair))
    aside = [functools.partial(unpack, i) for i in range(0, tiles, 2)]
    aside += [functools.partial(widen, i) for i in range(tiles - 1)]
    for k in range(tiles):
        f_ref[:, TILE : 2 * TILE] = eye
        factor(f_ref, w_ref, t_ref, aside)
        w = halves(w_ref[...])
        aside = []
        last = k == tiles - 1
        if not last:
            row_k = halves(a_ref[cut(k), (k + 1) * TILE : rank])
            near = halves(product(w, (row_k[0][:, 0:TILE], row_k[1][:, 0:TILE]), NN))
            f_ref[:, 0:TILE] = a_ref[cut(k + 1), cut(k + 1)] - product(near, near, TN)
            uh_ref[cut(k), cut(k + 1)], ul_ref[cut(k), cut(k + 1)] = near

        def spread(k=k, w=w):
            wide = slice((k + 2) * TILE, rank)
            uh_ref[cut(k), wide], ul_ref[cut(k), wide] = halves(
                product(w, halves(a_ref[cut(k), wide]), NN)
            )

        def solve(k=k, w=w, last=last):
            own = s_ref[:, cut(k)] if k == 0 else r_ref[:, cut(k)]
            if k == 0:
                q = lax.dot_general(own, w[0], (NT, ((), ())), preferred_element_type=f32)
                q = q + lax.dot_general(own, w[1], (NT, ((), ())), preferred_element_type=f32)
            else:
                q = product(halves(own), w, NT)
            out_ref[:, cut(k)] = (q * scale).astype(out_ref.dtype)
            if not last:
                r_ref[:, cut(k)] = q

        def trail(i, low, k=k):
            wide = slice(low * TILE, rank)
            a = (uh_ref[cut(k), cut(i)], ul_ref[cut(k), cut(i)])
            b = (uh_ref[cut(k), wide], ul_ref[cut(k), wide])
            a_ref[cut(i), wide] = a_ref[cut(i), wide] - product(a, b, TN)

        def carry(i, k=k):
            u = (uh_ref[cut(k), cut(i)], ul_ref[cut(k), cut(i)])
            own = s_ref[:, cut(i)].astype(f32) if k == 0 else r_ref[:, cut(i)]
            r_ref[:, cut(i)] = own - product(halves(r_ref[:, cut(k)]), u, NN)

        if last:
            solve()
        else:
            if k + 2 < tiles:
                aside.append(spread)
                aside.append(functools.partial(trail, k + 1, k + 2))
            for i in range(k + 2, tiles):
                aside.append(functools.partial(trail, i, i))
            aside.append(solve)
            for i in range(k + 1, tiles):
                aside.append(functools.partial(carry, i))


def whiten(gram, s, scale):
    rows, rank = s.shape
    return pl.pallas_call(
        functools.partial(whiten_kernel, scale),
        out_shape=jax.ShapeDtypeStruct((rows, rank), bf16),
        scratch_shapes=[
            pltpu.VMEM((rank, rank), f32),
            pltpu.VMEM((rows, rank), f32),
            pltpu.VMEM((TILE, 2 * TILE), f32),
            pltpu.VMEM((TILE, TILE), f32),
            pltpu.VMEM((2 * PANEL * PANEL, TILE), f32),
            pltpu.VMEM((rank, rank), bf16),
            pltpu.VMEM((rank, rank), bf16),
        ],
        compiler_params=pltpu.CompilerParams(vmem_limit_bytes=32 * 1024 * 1024),
    )(gram, s)


AXES = ("dir", "z", "y", "core")
PLANE = ("dir", "y", "core")


def scales_of(exponent_table):
    total = jnp.zeros(exponent_table.shape, jnp.float32)
    for exponent_value in range(-2, 3):
        total = total + jnp.where(
            exponent_table == exponent_value, jnp.float32(2.0**exponent_value), jnp.float32(0.0)
        )
    return total.astype(jnp.bfloat16)


def dequantize(values, exponent_table):
    height, breadth = values.shape
    edge_rows = height // exponent_table.shape[0]
    edge_cols = breadth // exponent_table.shape[1]
    scale_table = scales_of(exponent_table)
    tiled = values.reshape(exponent_table.shape[0], edge_rows, exponent_table.shape[1], edge_cols)
    tiled = tiled * scale_table[:, None, :, None]
    return tiled.reshape(height, breadth)


def listed(axes, sizes, shifts):
    names = tuple(sizes)
    ids = np.arange(math.prod(sizes.values())).reshape(tuple(sizes.values()))
    for name, shift in shifts.items():
        ids = np.roll(ids, -shift, axis=names.index(name))
    kept = [names.index(name) for name in names if name not in axes]
    ids = ids.transpose(kept + [names.index(name) for name in axes])
    width = math.prod(sizes[name] for name in axes)
    return [[int(i) for i in group] for group in ids.reshape(-1, width)]


def from_the_ends(group):
    half = len(group) // 2
    pairs = zip(group[half:], group[:half][::-1])
    return group[:1] + [device for pair in pairs for device in pair][:-1]


def exchange(pieces, groups):
    shape = pieces.shape
    paired = pieces.reshape(len(groups[0]), -1, 2, TILE)
    return lax.all_to_all(paired, AXES, 0, 0, axis_index_groups=groups).reshape(shape)


def sum_and_copy(pieces, count, copies):
    size = pieces.shape[0] // count
    chooser = jnp.asarray(np.tile(np.eye(size), (copies, count)), jnp.bfloat16)
    return jnp.dot(chooser, pieces, preferred_element_type=jnp.float32).astype(jnp.bfloat16)


def body(slab, exponents, sketch):
    scaled_values = dequantize(slab, exponents)
    partial_values = jnp.dot(scaled_values, sketch, preferred_element_type=jnp.float32)
    dirs, planes, depth = (lax.axis_size(axes) for axes in ("dir", PLANE, "z"))
    rank = sketch.shape[1]
    parts = partial_values.astype(jnp.bfloat16).reshape(dirs, -1, rank)
    parts = lax.all_to_all(parts, "dir", 0, 0)

    tiles = rank // TILE
    distinct = tiles * tiles // 2 * TILE + tiles // 2
    height = -(-distinct // (2 * planes)) * 2 * planes
    sketched, gram = local_gram(parts, height)
    sizes = {name: lax.axis_size(name) for name in AXES}
    flat = listed(PLANE, sizes, {"dir": dirs // 2, "y": sizes["y"] // 2})
    upright = listed(("z",), sizes, {"z": depth // 2})
    upright = [from_the_ends(group) for group in upright]
    gram = exchange(gram, flat)
    gram = exchange(sum_and_copy(gram, planes, depth), upright)
    gram = exchange(sum_and_copy(gram, depth, planes), flat)
    texel_count = sketched.shape[0] * planes * depth
    return whiten(gram, sketched, math.sqrt(texel_count))


def solution(mesh):
    fine = Mesh(mesh.devices.reshape(4, 16, 4, 2), ("dir", "z", "y", "core"))
    tex = ("z", "y", "core")
    return jax.shard_map(
        body,
        mesh=fine,
        in_specs=(P(tex, "dir"), P(tex, "dir"), P("dir", None)),
        out_specs=P(tex + ("dir",), None),
        check_vma=False,
    )
```

```python
import functools
import math

import jax
import jax.numpy as jnp
import numpy as np
from jax import lax
from jax.experimental import pallas as pl
from jax.experimental.pallas import tpu as pltpu
from jax.sharding import Mesh, PartitionSpec as P

f32 = jnp.float32
bf16 = jnp.bfloat16
TILE = 128
PANEL = 8
NN = ((1,), (0,))
TN = ((0,), (0,))
NT = ((1,), (1,))


def cut(i):
    return slice(i * TILE, (i + 1) * TILE)


def halves(x):
    high = x.astype(bf16)
    return high, (x - high.astype(f32)).astype(bf16)


def product(a, b, dims):
    def dot(x, y):
        return lax.dot_general(x, y, (dims, ((), ())), preferred_element_type=f32)

    return dot(a[0], b[0]) + (dot(a[0], b[1]) + dot(a[1], b[0]))


def places():
    shape = (TILE, TILE)
    return lax.broadcasted_iota(jnp.int32, shape, 0), lax.broadcasted_iota(jnp.int32, shape, 1)


def tree(terms):
    while len(terms) > 1:
        odd = terms[len(terms) // 2 * 2 :]
        terms = [terms[i] + terms[i + 1] for i in range(0, len(terms) - 1, 2)] + odd
    return terms[0]


def factor(a_ref, w_ref, t_ref, aside):
    shape = (PANEL, TILE)
    sub = lax.broadcasted_iota(jnp.int32, shape, 0)
    lane = lax.broadcasted_iota(jnp.int32, shape, 1)
    steps = TILE // PANEL
    pa, pm = a_ref[0:PANEL, 0:TILE], a_ref[0:PANEL, TILE : 2 * TILE]
    for p in range(steps):
        at, after = p * PANEL, (p + 1) * PANEL
        base = p % 2 * PANEL * PANEL
        for j in range(PANEL):
            spread = jnp.broadcast_to(pa[:, at + j : at + j + 1], shape)
            t_ref[base + PANEL * j : base + PANEL * (j + 1), :] = spread
        e = [
            [t_ref[pl.ds(base + PANEL * j + i, PANEL, stride=0), :] for j in range(i + 1)]
            for i in range(PANEL)
        ]
        ua = [jnp.broadcast_to(pa[i : i + 1, :], shape) for i in range(PANEL)]
        um = [jnp.broadcast_to(pm[i : i + 1, :], shape) for i in range(PANEL)]
        more = p < steps - 1
        if more:
            here = lane == after + sub
            nxt = [
                jnp.broadcast_to(
                    jnp.sum(jnp.where(here, ua[j], 0.0), axis=1, keepdims=True), shape
                )
                for j in range(PANEL)
            ]
        inv = []
        for j in range(PANEL):
            inv.append(pl.reciprocal(e[j][j], approx=True))
            for i in range(j + 1, PANEL):
                ratio = e[i][j] * inv[j]
                for k in range(j + 1, i + 1):
                    e[i][k] = e[i][k] - ratio * e[k][j]
                ua[i] = ua[i] - ratio * ua[j]
                um[i] = um[i] - ratio * um[j]
                if more:
                    nxt[i] = nxt[i] - ratio * nxt[j]
        if more:
            weights = [nxt[j] * inv[j] for j in range(PANEL)]
            rows = slice(after, after + PANEL)
            pa = a_ref[rows, 0:TILE] - tree([w * u for w, u in zip(weights, ua)])
            pm = a_ref[rows, TILE : 2 * TILE] - tree([w * u for w, u in zip(weights, um)])
        outa, outm, pivots = ua[0], um[0], e[0][0]
        for i in range(1, PANEL):
            outa = jnp.where(sub == i, ua[i], outa)
            outm = jnp.where(sub == i, um[i], outm)
            pivots = jnp.where(sub == i, e[i][i], pivots)
        root = lax.rsqrt(pivots)
        outa, outm = outa * root, outm * root
        w_ref[at:after, :] = outm
        if aside:
            aside.pop(0)()
        rest = after + PANEL
        if rest < TILE:
            lowa = outa - outa.astype(bf16).astype(f32)
            lowm = outm - outm.astype(bf16).astype(f32)
            none = jnp.zeros(shape, f32)
            high = jnp.concatenate([outa, outm], axis=1)
            low = jnp.concatenate([lowa, lowm], axis=1)
            left = jnp.concatenate([outa, outa, lowa, none], axis=0).astype(bf16)
            right = jnp.concatenate([high, low, high, jnp.zeros_like(low)], axis=0).astype(bf16)
            update = lax.dot_general(left, right, (TN, ((), ())), preferred_element_type=f32)
            a_ref[rest:TILE, :] = a_ref[rest:TILE, :] - update[rest:TILE, :]
    while aside:
        aside.pop(0)()


def gram_kernel(parts_ref, s_ref, gram_ref):
    total = parts_ref[0].astype(f32)
    for g in range(1, parts_ref.shape[0]):
        total = total + parts_ref[g].astype(f32)
    s_ref[...] = total.astype(bf16)
    rank = s_ref.shape[1]
    tiles = rank // TILE
    row, col = places()
    at = tiles // 2
    diagonal = []
    for i in range(tiles):
        strip = lax.dot_general(
            s_ref[:, cut(i)],
            s_ref[:, i * TILE : rank],
            (TN, ((), ())),
            preferred_element_type=f32,
        )
        diagonal.append(strip[:, 0:TILE])
        for j in range(1, tiles - i):
            gram_ref[cut(at), :] = strip[:, cut(j)].astype(bf16)
            at += 1
    tail = []
    for i in range(0, tiles, 2):
        gram_ref[cut(i // 2), :] = jnp.where(col >= row, diagonal[i], diagonal[i + 1]).astype(bf16)
        tail.append(jnp.sum(jnp.where(row == col, diagonal[i + 1], 0.0), axis=0, keepdims=True))
    rest = gram_ref.shape[0] - at * TILE
    tail.append(jnp.zeros((rest - len(tail), TILE), f32))
    gram_ref[at * TILE : at * TILE + rest, :] = jnp.concatenate(tail, axis=0).astype(bf16)


def local_gram(parts, height):
    rows, rank = parts.shape[1:]
    return pl.pallas_call(
        gram_kernel,
        out_shape=(
            jax.ShapeDtypeStruct((rows, rank), bf16),
            jax.ShapeDtypeStruct((height, TILE), bf16),
        ),
        compiler_params=pltpu.CompilerParams(vmem_limit_bytes=32 * 1024 * 1024),
    )(parts)


def whiten_kernel(scale, gram_ref, s_ref, out_ref, a_ref, r_ref, f_ref, w_ref, t_ref, uh_ref, ul_ref):
    rank = s_ref.shape[1]
    tiles = rank // TILE
    row, col = places()
    eye = jnp.where(row == col, 1.0, 0.0)
    across = tiles // 2
    offset = (across + tiles * (tiles - 1) // 2) * TILE

    def unpack(i):
        pair = gram_ref[cut(i // 2), :].astype(f32)
        turned = jnp.transpose(pair)
        tail = gram_ref[offset : offset + 16, :].astype(f32)
        second = jnp.where(col < row, pair, turned)
        second = jnp.where(row == col, tail[i // 2 : i // 2 + 1, :], second)
        if i > 0:
            a_ref[cut(i), cut(i)] = jnp.where(col >= row, pair, turned)
        a_ref[cut(i + 1), cut(i + 1)] = second

    def widen(i):
        start = across + i * (tiles - 1) - i * (i - 1) // 2
        for j in range(i + 1, tiles):
            a_ref[cut(i), cut(j)] = gram_ref[cut(start + j - i - 1), :].astype(f32)

    pair = gram_ref[cut(0), :].astype(f32)
    f_ref[:, 0:TILE] = jnp.where(col >= row, pair, jnp.transpose(pair))
    aside = [functools.partial(unpack, i) for i in range(0, tiles, 2)]
    aside += [functools.partial(widen, i) for i in range(tiles - 1)]
    for k in range(tiles):
        f_ref[:, TILE : 2 * TILE] = eye
        factor(f_ref, w_ref, t_ref, aside)
        w = halves(w_ref[...])
        aside = []
        last = k == tiles - 1
        if not last:
            row_k = halves(a_ref[cut(k), (k + 1) * TILE : rank])
            near = halves(product(w, (row_k[0][:, 0:TILE], row_k[1][:, 0:TILE]), NN))
            f_ref[:, 0:TILE] = a_ref[cut(k + 1), cut(k + 1)] - product(near, near, TN)
            uh_ref[cut(k), cut(k + 1)], ul_ref[cut(k), cut(k + 1)] = near

        def spread(k=k, w=w):
            wide = slice((k + 2) * TILE, rank)
            uh_ref[cut(k), wide], ul_ref[cut(k), wide] = halves(
                product(w, halves(a_ref[cut(k), wide]), NN)
            )

        def solve(k=k, w=w, last=last):
            own = s_ref[:, cut(k)] if k == 0 else r_ref[:, cut(k)]
            if k == 0:
                q = lax.dot_general(own, w[0], (NT, ((), ())), preferred_element_type=f32)
                q = q + lax.dot_general(own, w[1], (NT, ((), ())), preferred_element_type=f32)
            else:
                q = product(halves(own), w, NT)
            out_ref[:, cut(k)] = (q * scale).astype(out_ref.dtype)
            if not last:
                r_ref[:, cut(k)] = q

        def trail(i, low, k=k):
            wide = slice(low * TILE, rank)
            a = (uh_ref[cut(k), cut(i)], ul_ref[cut(k), cut(i)])
            b = (uh_ref[cut(k), wide], ul_ref[cut(k), wide])
            a_ref[cut(i), wide] = a_ref[cut(i), wide] - product(a, b, TN)

        def carry(i, k=k):
            u = (uh_ref[cut(k), cut(i)], ul_ref[cut(k), cut(i)])
            own = s_ref[:, cut(i)].astype(f32) if k == 0 else r_ref[:, cut(i)]
            r_ref[:, cut(i)] = own - product(halves(r_ref[:, cut(k)]), u, NN)

        if last:
            solve()
        else:
            if k + 2 < tiles:
                aside.append(spread)
                aside.append(functools.partial(trail, k + 1, k + 2))
            for i in range(k + 2, tiles):
                aside.append(functools.partial(trail, i, i))
            aside.append(solve)
            for i in range(k + 1, tiles):
                aside.append(functools.partial(carry, i))


def whiten(gram, s, scale):
    rows, rank = s.shape
    return pl.pallas_call(
        functools.partial(whiten_kernel, scale),
        out_shape=jax.ShapeDtypeStruct((rows, rank), bf16),
        scratch_shapes=[
            pltpu.VMEM((rank, rank), f32),
            pltpu.VMEM((rows, rank), f32),
            pltpu.VMEM((TILE, 2 * TILE), f32),
            pltpu.VMEM((TILE, TILE), f32),
            pltpu.VMEM((2 * PANEL * PANEL, TILE), f32),
            pltpu.VMEM((rank, rank), bf16),
            pltpu.VMEM((rank, rank), bf16),
        ],
        compiler_params=pltpu.CompilerParams(vmem_limit_bytes=32 * 1024 * 1024),
    )(gram, s)


AXES = ("dir", "z", "y", "core")
PLANE = ("core", "dir", "y")


def scales_of(exponent_table):
    total = jnp.zeros(exponent_table.shape, jnp.float32)
    for exponent_value in range(-2, 3):
        total = total + jnp.where(
            exponent_table == exponent_value, jnp.float32(2.0**exponent_value), jnp.float32(0.0)
        )
    return total.astype(jnp.bfloat16)


def dequantize(values, exponent_table):
    height, breadth = values.shape
    edge_rows = height // exponent_table.shape[0]
    edge_cols = breadth // exponent_table.shape[1]
    scale_table = scales_of(exponent_table)
    tiled = values.reshape(exponent_table.shape[0], edge_rows, exponent_table.shape[1], edge_cols)
    tiled = tiled * scale_table[:, None, :, None]
    return tiled.reshape(height, breadth)


def listed(axes, sizes, shifts):
    names = tuple(sizes)
    ids = np.arange(math.prod(sizes.values())).reshape(tuple(sizes.values()))
    for name, shift in shifts.items():
        ids = np.roll(ids, -shift, axis=names.index(name))
    kept = [names.index(name) for name in names if name not in axes]
    ids = ids.transpose(kept + [names.index(name) for name in axes])
    width = math.prod(sizes[name] for name in axes)
    return [[int(i) for i in group] for group in ids.reshape(-1, width)]


def from_the_ends(group):
    half = len(group) // 2
    pairs = zip(group[half:], group[:half][::-1])
    return group[:1] + [device for pair in pairs for device in pair][:-1]


def exchange(pieces, groups):
    shape = pieces.shape
    paired = pieces.reshape(len(groups[0]), -1, 2, TILE)
    return lax.all_to_all(paired, AXES, 0, 0, axis_index_groups=groups).reshape(shape)


def sum_and_copy(pieces, count, copies):
    size = pieces.shape[0] // count
    chooser = jnp.asarray(np.tile(np.eye(size), (copies, count)), jnp.bfloat16)
    return jnp.dot(chooser, pieces, preferred_element_type=jnp.float32).astype(jnp.bfloat16)


def body(slab, exponents, sketch):
    scaled_values = dequantize(slab, exponents)
    partial_values = jnp.dot(scaled_values, sketch, preferred_element_type=jnp.float32)
    dirs, planes, depth = (lax.axis_size(axes) for axes in ("dir", PLANE, "z"))
    rank = sketch.shape[1]
    parts = partial_values.astype(jnp.bfloat16).reshape(dirs, -1, rank)
    sizes = {name: lax.axis_size(name) for name in AXES}
    middle = {name: sizes[name] // 2 for name in AXES[:-1]}
    parts = jnp.roll(parts, -middle["dir"], axis=0)
    row = listed(("dir",), sizes, {"dir": middle["dir"]})
    parts = lax.all_to_all(parts, AXES, 0, 0, axis_index_groups=row)

    tiles = rank // TILE
    distinct = tiles * tiles // 2 * TILE + tiles // 2
    height = -(-distinct // (2 * planes)) * 2 * planes
    sketched, gram = local_gram(parts, height)
    flat = listed(PLANE, sizes, {"dir": middle["dir"], "y": middle["y"]})
    upright = listed(("z",), sizes, {"z": middle["z"]})
    upright = [from_the_ends(group) for group in upright]
    gram = exchange(gram, flat)
    gram = exchange(sum_and_copy(gram, planes, depth), upright)
    gram = exchange(sum_and_copy(gram, depth, planes), flat)
    texel_count = sketched.shape[0] * planes * depth
    return whiten(gram, sketched, math.sqrt(texel_count))


def solution(mesh):
    fine = Mesh(mesh.devices.reshape(4, 16, 4, 2), ("dir", "z", "y", "core"))
    tex = ("z", "y", "core")
    return jax.shard_map(
        body,
        mesh=fine,
        in_specs=(P(tex, "dir"), P(tex, "dir"), P("dir", None)),
        out_specs=P(tex + ("dir",), None),
        check_vma=False,
    )
```

```python
import functools
import math

import jax
import jax.numpy as jnp
import numpy as np
from jax import lax
from jax.experimental import pallas as pl
from jax.experimental.pallas import tpu as pltpu
from jax.sharding import Mesh, PartitionSpec as P

f32 = jnp.float32
bf16 = jnp.bfloat16
TILE = 128
PANEL = 8
NN = ((1,), (0,))
TN = ((0,), (0,))
NT = ((1,), (1,))


def cut(i):
    return slice(i * TILE, (i + 1) * TILE)


def halves(x):
    high = x.astype(bf16)
    return high, (x - high.astype(f32)).astype(bf16)


def product(a, b, dims):
    left = jnp.concatenate([a[0], a[0], a[1]], axis=dims[0][0])
    right = jnp.concatenate([b[0], b[1], b[0]], axis=dims[1][0])
    return lax.dot_general(left, right, (dims, ((), ())), preferred_element_type=f32)


def places():
    shape = (TILE, TILE)
    return lax.broadcasted_iota(jnp.int32, shape, 0), lax.broadcasted_iota(jnp.int32, shape, 1)


def tree(terms):
    while len(terms) > 1:
        odd = terms[len(terms) // 2 * 2 :]
        terms = [terms[i] + terms[i + 1] for i in range(0, len(terms) - 1, 2)] + odd
    return terms[0]


def factor(a_ref, w_ref, t_ref, aside):
    shape = (PANEL, TILE)
    sub = lax.broadcasted_iota(jnp.int32, shape, 0)
    lane = lax.broadcasted_iota(jnp.int32, shape, 1)
    steps = TILE // PANEL
    pa, pm = a_ref[0:PANEL, 0:TILE], a_ref[0:PANEL, TILE : 2 * TILE]
    for p in range(steps):
        at, after = p * PANEL, (p + 1) * PANEL
        base = p % 2 * PANEL * PANEL
        for j in range(PANEL):
            spread = jnp.broadcast_to(pa[:, at + j : at + j + 1], shape)
            t_ref[base + PANEL * j : base + PANEL * (j + 1), :] = spread
        e = [
            [t_ref[pl.ds(base + PANEL * j + i, PANEL, stride=0), :] for j in range(i + 1)]
            for i in range(PANEL)
        ]
        ua = [jnp.broadcast_to(pa[i : i + 1, :], shape) for i in range(PANEL)]
        um = [jnp.broadcast_to(pm[i : i + 1, :], shape) for i in range(PANEL)]
        more = p < steps - 1
        if more:
            here = lane == after + sub
            nxt = [
                jnp.broadcast_to(
                    jnp.sum(jnp.where(here, ua[j], 0.0), axis=1, keepdims=True), shape
                )
                for j in range(PANEL)
            ]
        inv = []
        for j in range(PANEL):
            inv.append(pl.reciprocal(e[j][j], approx=True))
            for i in range(j + 1, PANEL):
                ratio = e[i][j] * inv[j]
                for k in range(j + 1, i + 1):
                    e[i][k] = e[i][k] - ratio * e[k][j]
                ua[i] = ua[i] - ratio * ua[j]
                um[i] = um[i] - ratio * um[j]
                if more:
                    nxt[i] = nxt[i] - ratio * nxt[j]
        if more:
            weights = [nxt[j] * inv[j] for j in range(PANEL)]
            rows = slice(after, after + PANEL)
            pa = a_ref[rows, 0:TILE] - tree([w * u for w, u in zip(weights, ua)])
            pm = a_ref[rows, TILE : 2 * TILE] - tree([w * u for w, u in zip(weights, um)])
        outa, outm, pivots = ua[0], um[0], e[0][0]
        for i in range(1, PANEL):
            outa = jnp.where(sub == i, ua[i], outa)
            outm = jnp.where(sub == i, um[i], outm)
            pivots = jnp.where(sub == i, e[i][i], pivots)
        root = lax.rsqrt(pivots)
        outa, outm = outa * root, outm * root
        w_ref[at:after, :] = outm
        if aside:
            aside.pop(0)()
        rest = after + PANEL
        if rest < TILE:
            lowa = outa - outa.astype(bf16).astype(f32)
            lowm = outm - outm.astype(bf16).astype(f32)
            none = jnp.zeros(shape, f32)
            high = jnp.concatenate([outa, outm], axis=1)
            low = jnp.concatenate([lowa, lowm], axis=1)
            left = jnp.concatenate([outa, outa, lowa, none], axis=0).astype(bf16)
            right = jnp.concatenate([high, low, high, jnp.zeros_like(low)], axis=0).astype(bf16)
            update = lax.dot_general(left, right, (TN, ((), ())), preferred_element_type=f32)
            a_ref[rest:TILE, :] = a_ref[rest:TILE, :] - update[rest:TILE, :]
    while aside:
        aside.pop(0)()


def gram_kernel(parts_ref, s_ref, gram_ref):
    total = parts_ref[0].astype(f32)
    for g in range(1, parts_ref.shape[0]):
        total = total + parts_ref[g].astype(f32)
    s_ref[...] = total.astype(bf16)
    rank = s_ref.shape[1]
    tiles = rank // TILE
    row, col = places()
    at = tiles // 2
    diagonal = []
    for i in range(tiles):
        strip = lax.dot_general(
            s_ref[:, cut(i)],
            s_ref[:, i * TILE : rank],
            (TN, ((), ())),
            preferred_element_type=f32,
        )
        diagonal.append(strip[:, 0:TILE])
        for j in range(1, tiles - i):
            gram_ref[cut(at), :] = strip[:, cut(j)].astype(bf16)
            at += 1
    tail = []
    for i in range(0, tiles, 2):
        gram_ref[cut(i // 2), :] = jnp.where(col >= row, diagonal[i], diagonal[i + 1]).astype(bf16)
        tail.append(jnp.sum(jnp.where(row == col, diagonal[i + 1], 0.0), axis=0, keepdims=True))
    rest = gram_ref.shape[0] - at * TILE
    tail.append(jnp.zeros((rest - len(tail), TILE), f32))
    gram_ref[at * TILE : at * TILE + rest, :] = jnp.concatenate(tail, axis=0).astype(bf16)


def local_gram(parts, height):
    rows, rank = parts.shape[1:]
    return pl.pallas_call(
        gram_kernel,
        out_shape=(
            jax.ShapeDtypeStruct((rows, rank), bf16),
            jax.ShapeDtypeStruct((height, TILE), bf16),
        ),
        compiler_params=pltpu.CompilerParams(vmem_limit_bytes=32 * 1024 * 1024),
    )(parts)


def whiten_kernel(scale, gram_ref, s_ref, out_ref, a_ref, r_ref, f_ref, w_ref, t_ref, uh_ref, ul_ref):
    rank = s_ref.shape[1]
    tiles = rank // TILE
    row, col = places()
    eye = jnp.where(row == col, 1.0, 0.0)
    across = tiles // 2
    offset = (across + tiles * (tiles - 1) // 2) * TILE

    def unpack(i):
        pair = gram_ref[cut(i // 2), :].astype(f32)
        turned = jnp.transpose(pair)
        tail = gram_ref[offset : offset + 16, :].astype(f32)
        second = jnp.where(col < row, pair, turned)
        second = jnp.where(row == col, tail[i // 2 : i // 2 + 1, :], second)
        if i > 0:
            a_ref[cut(i), cut(i)] = jnp.where(col >= row, pair, turned)
        a_ref[cut(i + 1), cut(i + 1)] = second

    def widen(i):
        start = across + i * (tiles - 1) - i * (i - 1) // 2
        for j in range(i + 1, tiles):
            a_ref[cut(i), cut(j)] = gram_ref[cut(start + j - i - 1), :].astype(f32)

    pair = gram_ref[cut(0), :].astype(f32)
    f_ref[:, 0:TILE] = jnp.where(col >= row, pair, jnp.transpose(pair))
    aside = [functools.partial(unpack, i) for i in range(0, tiles, 2)]
    aside += [functools.partial(widen, i) for i in range(tiles - 1)]
    for k in range(tiles):
        f_ref[:, TILE : 2 * TILE] = eye
        factor(f_ref, w_ref, t_ref, aside)
        w = halves(w_ref[...])
        aside = []
        last = k == tiles - 1
        if not last:
            row_k = halves(a_ref[cut(k), (k + 1) * TILE : rank])
            near = halves(product(w, (row_k[0][:, 0:TILE], row_k[1][:, 0:TILE]), NN))
            f_ref[:, 0:TILE] = a_ref[cut(k + 1), cut(k + 1)] - product(near, near, TN)
            uh_ref[cut(k), cut(k + 1)], ul_ref[cut(k), cut(k + 1)] = near

        def spread(k=k, w=w):
            wide = slice((k + 2) * TILE, rank)
            uh_ref[cut(k), wide], ul_ref[cut(k), wide] = halves(
                product(w, halves(a_ref[cut(k), wide]), NN)
            )

        def solve(k=k, w=w, last=last):
            own = s_ref[:, cut(k)] if k == 0 else r_ref[:, cut(k)]
            if k == 0:
                q = lax.dot_general(own, w[0], (NT, ((), ())), preferred_element_type=f32)
                q = q + lax.dot_general(own, w[1], (NT, ((), ())), preferred_element_type=f32)
            else:
                q = product(halves(own), w, NT)
            out_ref[:, cut(k)] = (q * scale).astype(out_ref.dtype)
            if not last:
                r_ref[:, cut(k)] = q

        def trail(i, low, k=k):
            wide = slice(low * TILE, rank)
            a = (uh_ref[cut(k), cut(i)], ul_ref[cut(k), cut(i)])
            b = (uh_ref[cut(k), wide], ul_ref[cut(k), wide])
            a_ref[cut(i), wide] = a_ref[cut(i), wide] - product(a, b, TN)

        def carry(i, k=k):
            u = (uh_ref[cut(k), cut(i)], ul_ref[cut(k), cut(i)])
            own = s_ref[:, cut(i)].astype(f32) if k == 0 else r_ref[:, cut(i)]
            r_ref[:, cut(i)] = own - product(halves(r_ref[:, cut(k)]), u, NN)

        if last:
            solve()
        else:
            if k + 2 < tiles:
                aside.append(spread)
                aside.append(functools.partial(trail, k + 1, k + 2))
            for i in range(k + 2, tiles):
                aside.append(functools.partial(trail, i, i))
            aside.append(solve)
            for i in range(k + 1, tiles):
                aside.append(functools.partial(carry, i))


def whiten(gram, s, scale):
    rows, rank = s.shape
    return pl.pallas_call(
        functools.partial(whiten_kernel, scale),
        out_shape=jax.ShapeDtypeStruct((rows, rank), bf16),
        scratch_shapes=[
            pltpu.VMEM((rank, rank), f32),
            pltpu.VMEM((rows, rank), f32),
            pltpu.VMEM((TILE, 2 * TILE), f32),
            pltpu.VMEM((TILE, TILE), f32),
            pltpu.VMEM((2 * PANEL * PANEL, TILE), f32),
            pltpu.VMEM((rank, rank), bf16),
            pltpu.VMEM((rank, rank), bf16),
        ],
        compiler_params=pltpu.CompilerParams(vmem_limit_bytes=32 * 1024 * 1024),
    )(gram, s)


AXES = ("dir", "z", "y", "core")
PLANE = ("core", "dir", "y")


def scales_of(exponent_table):
    total = jnp.zeros(exponent_table.shape, jnp.float32)
    for exponent_value in range(-2, 3):
        total = total + jnp.where(
            exponent_table == exponent_value, jnp.float32(2.0**exponent_value), jnp.float32(0.0)
        )
    return total.astype(jnp.bfloat16)


def dequantize(values, exponent_table):
    height, breadth = values.shape
    edge_rows = height // exponent_table.shape[0]
    edge_cols = breadth // exponent_table.shape[1]
    scale_table = scales_of(exponent_table)
    tiled = values.reshape(exponent_table.shape[0], edge_rows, exponent_table.shape[1], edge_cols)
    tiled = tiled * scale_table[:, None, :, None]
    return tiled.reshape(height, breadth)


def listed(axes, sizes, shifts):
    names = tuple(sizes)
    ids = np.arange(math.prod(sizes.values())).reshape(tuple(sizes.values()))
    for name, shift in shifts.items():
        ids = np.roll(ids, -shift, axis=names.index(name))
    kept = [names.index(name) for name in names if name not in axes]
    ids = ids.transpose(kept + [names.index(name) for name in axes])
    width = math.prod(sizes[name] for name in axes)
    return [[int(i) for i in group] for group in ids.reshape(-1, width)]


def from_the_ends(group):
    half = len(group) // 2
    pairs = zip(group[half:], group[:half][::-1])
    return group[:1] + [device for pair in pairs for device in pair][:-1]


def exchange(pieces, groups):
    shape = pieces.shape
    paired = pieces.reshape(len(groups[0]), -1, 2, TILE)
    return lax.all_to_all(paired, AXES, 0, 0, axis_index_groups=groups).reshape(shape)


def sum_and_copy(pieces, count, copies):
    size = pieces.shape[0] // count
    chooser = jnp.asarray(np.tile(np.eye(size), (copies, count)), jnp.bfloat16)
    return jnp.dot(chooser, pieces, preferred_element_type=jnp.float32).astype(jnp.bfloat16)


def body(slab, exponents, sketch):
    scaled_values = dequantize(slab, exponents)
    partial_values = jnp.dot(scaled_values, sketch, preferred_element_type=jnp.float32)
    dirs, planes, depth = (lax.axis_size(axes) for axes in ("dir", PLANE, "z"))
    rank = sketch.shape[1]
    parts = partial_values.astype(jnp.bfloat16).reshape(dirs, -1, rank)
    sizes = {name: lax.axis_size(name) for name in AXES}
    middle = {name: sizes[name] // 2 for name in AXES[:-1]}
    parts = jnp.roll(parts, -middle["dir"], axis=0)
    row = listed(("dir",), sizes, {"dir": middle["dir"]})
    parts = lax.all_to_all(parts, AXES, 0, 0, axis_index_groups=row)

    tiles = rank // TILE
    distinct = tiles * tiles // 2 * TILE + tiles // 2
    height = -(-distinct // (2 * planes)) * 2 * planes
    sketched, gram = local_gram(parts, height)
    flat = listed(PLANE, sizes, {"dir": middle["dir"], "y": middle["y"], "core": 1})
    upright = listed(("z",), sizes, {"z": middle["z"]})
    upright = [from_the_ends(group) for group in upright]
    gram = exchange(gram, flat)
    gram = exchange(sum_and_copy(gram, planes, depth), upright)
    gram = exchange(sum_and_copy(gram, depth, planes), flat)
    texel_count = sketched.shape[0] * planes * depth
    return whiten(gram, sketched, math.sqrt(texel_count))


def solution(mesh):
    fine = Mesh(mesh.devices.reshape(4, 16, 4, 2), ("dir", "z", "y", "core"))
    tex = ("z", "y", "core")
    return jax.shard_map(
        body,
        mesh=fine,
        in_specs=(P(tex, "dir"), P(tex, "dir"), P("dir", None)),
        out_specs=P(tex + ("dir",), None),
        check_vma=False,
    )
```

```python
import functools
import math

import jax
import jax.numpy as jnp
import numpy as np
from jax import lax
from jax.experimental import pallas as pl
from jax.experimental.pallas import tpu as pltpu
from jax.sharding import Mesh, PartitionSpec as P

f32 = jnp.float32
bf16 = jnp.bfloat16
TILE = 128
PANEL = 8
NN = ((1,), (0,))
TN = ((0,), (0,))
NT = ((1,), (1,))


def cut(i):
    return slice(i * TILE, (i + 1) * TILE)


def halves(x):
    high = x.astype(bf16)
    return high, (x - high.astype(f32)).astype(bf16)


def product(a, b, dims):
    left = jnp.concatenate([a[0], a[0], a[1]], axis=dims[0][0])
    right = jnp.concatenate([b[0], b[1], b[0]], axis=dims[1][0])
    return lax.dot_general(left, right, (dims, ((), ())), preferred_element_type=f32)


def places():
    shape = (TILE, TILE)
    return lax.broadcasted_iota(jnp.int32, shape, 0), lax.broadcasted_iota(jnp.int32, shape, 1)


def tree(terms):
    while len(terms) > 1:
        odd = terms[len(terms) // 2 * 2 :]
        terms = [terms[i] + terms[i + 1] for i in range(0, len(terms) - 1, 2)] + odd
    return terms[0]


def factor(a_ref, w_ref, t_ref, aside):
    shape = (PANEL, TILE)
    sub = lax.broadcasted_iota(jnp.int32, shape, 0)
    lane = lax.broadcasted_iota(jnp.int32, shape, 1)
    steps = TILE // PANEL
    pa, pm = a_ref[0:PANEL, 0:TILE], a_ref[0:PANEL, TILE : 2 * TILE]
    for p in range(steps):
        at, after = p * PANEL, (p + 1) * PANEL
        base = p % 2 * PANEL * PANEL
        for j in range(PANEL):
            spread = jnp.broadcast_to(pa[:, at + j : at + j + 1], shape)
            t_ref[base + PANEL * j : base + PANEL * (j + 1), :] = spread
        e = [
            [t_ref[pl.ds(base + PANEL * j + i, PANEL, stride=0), :] for j in range(i + 1)]
            for i in range(PANEL)
        ]
        ua = [jnp.broadcast_to(pa[i : i + 1, :], shape) for i in range(PANEL)]
        um = [jnp.broadcast_to(pm[i : i + 1, :], shape) for i in range(PANEL)]
        more = p < steps - 1
        if more:
            here = lane == after + sub
            nxt = [
                jnp.broadcast_to(
                    jnp.sum(jnp.where(here, ua[j], 0.0), axis=1, keepdims=True), shape
                )
                for j in range(PANEL)
            ]
        inv = []
        for j in range(PANEL):
            inv.append(pl.reciprocal(e[j][j], approx=True))
            for i in range(j + 1, PANEL):
                ratio = e[i][j] * inv[j]
                for k in range(j + 1, i + 1):
                    e[i][k] = e[i][k] - ratio * e[k][j]
                ua[i] = ua[i] - ratio * ua[j]
                um[i] = um[i] - ratio * um[j]
                if more:
                    nxt[i] = nxt[i] - ratio * nxt[j]
        if more:
            weights = [nxt[j] * inv[j] for j in range(PANEL)]
            rows = slice(after, after + PANEL)
            pa = a_ref[rows, 0:TILE] - tree([w * u for w, u in zip(weights, ua)])
            pm = a_ref[rows, TILE : 2 * TILE] - tree([w * u for w, u in zip(weights, um)])
        outa, outm, pivots = ua[0], um[0], e[0][0]
        for i in range(1, PANEL):
            outa = jnp.where(sub == i, ua[i], outa)
            outm = jnp.where(sub == i, um[i], outm)
            pivots = jnp.where(sub == i, e[i][i], pivots)
        root = lax.rsqrt(pivots)
        outa, outm = outa * root, outm * root
        w_ref[at:after, :] = outm
        if aside:
            aside.pop(0)()
        rest = after + PANEL
        if rest < TILE:
            lowa = outa - outa.astype(bf16).astype(f32)
            lowm = outm - outm.astype(bf16).astype(f32)
            none = jnp.zeros(shape, f32)
            high = jnp.concatenate([outa, outm], axis=1)
            low = jnp.concatenate([lowa, lowm], axis=1)
            left = jnp.concatenate([outa, outa, lowa, none], axis=0).astype(bf16)
            right = jnp.concatenate([high, low, high, jnp.zeros_like(low)], axis=0).astype(bf16)
            update = lax.dot_general(left, right, (TN, ((), ())), preferred_element_type=f32)
            a_ref[rest:TILE, :] = a_ref[rest:TILE, :] - update[rest:TILE, :]
    while aside:
        aside.pop(0)()


def gram_kernel(parts_ref, s_ref, gram_ref):
    total = parts_ref[0].astype(f32)
    for g in range(1, parts_ref.shape[0]):
        total = total + parts_ref[g].astype(f32)
    s_ref[...] = total.astype(bf16)
    rank = s_ref.shape[1]
    tiles = rank // TILE
    row, col = places()
    at = tiles // 2
    diagonal = []
    for i in range(tiles):
        strip = lax.dot_general(
            s_ref[:, cut(i)],
            s_ref[:, i * TILE : rank],
            (TN, ((), ())),
            preferred_element_type=f32,
        )
        diagonal.append(strip[:, 0:TILE])
        for j in range(1, tiles - i):
            gram_ref[cut(at), :] = strip[:, cut(j)].astype(bf16)
            at += 1
    tail = []
    for i in range(0, tiles, 2):
        gram_ref[cut(i // 2), :] = jnp.where(col >= row, diagonal[i], diagonal[i + 1]).astype(bf16)
        tail.append(jnp.sum(jnp.where(row == col, diagonal[i + 1], 0.0), axis=0, keepdims=True))
    rest = gram_ref.shape[0] - at * TILE
    tail.append(jnp.zeros((rest - len(tail), TILE), f32))
    gram_ref[at * TILE : at * TILE + rest, :] = jnp.concatenate(tail, axis=0).astype(bf16)


def local_gram(parts, height):
    rows, rank = parts.shape[1:]
    return pl.pallas_call(
        gram_kernel,
        out_shape=(
            jax.ShapeDtypeStruct((rows, rank), bf16),
            jax.ShapeDtypeStruct((height, TILE), bf16),
        ),
        compiler_params=pltpu.CompilerParams(vmem_limit_bytes=32 * 1024 * 1024),
    )(parts)


def whiten_kernel(scale, gram_ref, s_ref, out_ref, a_ref, r_ref, f_ref, w_ref, t_ref, uh_ref, ul_ref):
    rank = s_ref.shape[1]
    tiles = rank // TILE
    row, col = places()
    eye = jnp.where(row == col, 1.0, 0.0)
    across = tiles // 2
    offset = (across + tiles * (tiles - 1) // 2) * TILE

    def unpack(i):
        pair = gram_ref[cut(i // 2), :].astype(f32)
        turned = jnp.transpose(pair)
        tail = gram_ref[offset : offset + 16, :].astype(f32)
        second = jnp.where(col < row, pair, turned)
        second = jnp.where(row == col, tail[i // 2 : i // 2 + 1, :], second)
        if i > 0:
            a_ref[cut(i), cut(i)] = jnp.where(col >= row, pair, turned)
        a_ref[cut(i + 1), cut(i + 1)] = second

    def widen(i):
        start = across + i * (tiles - 1) - i * (i - 1) // 2
        for j in range(i + 1, tiles):
            a_ref[cut(i), cut(j)] = gram_ref[cut(start + j - i - 1), :].astype(f32)

    pair = gram_ref[cut(0), :].astype(f32)
    f_ref[:, 0:TILE] = jnp.where(col >= row, pair, jnp.transpose(pair))
    aside = [functools.partial(unpack, i) for i in range(0, tiles, 2)]
    aside += [functools.partial(widen, i) for i in range(tiles - 1)]
    for k in range(tiles):
        f_ref[:, TILE : 2 * TILE] = eye
        factor(f_ref, w_ref, t_ref, aside)
        w = halves(w_ref[...])
        aside = []
        last = k == tiles - 1
        if not last:
            row_k = halves(a_ref[cut(k), (k + 1) * TILE : rank])
            near = halves(product(w, (row_k[0][:, 0:TILE], row_k[1][:, 0:TILE]), NN))
            f_ref[:, 0:TILE] = a_ref[cut(k + 1), cut(k + 1)] - product(near, near, TN)
            uh_ref[cut(k), cut(k + 1)], ul_ref[cut(k), cut(k + 1)] = near

        def spread(k=k, w=w):
            wide = slice((k + 2) * TILE, rank)
            uh_ref[cut(k), wide], ul_ref[cut(k), wide] = halves(
                product(w, halves(a_ref[cut(k), wide]), NN)
            )

        def solve(k=k, w=w, last=last):
            own = s_ref[:, cut(k)] if k == 0 else r_ref[:, cut(k)]
            if k == 0:
                q = lax.dot_general(own, w[0], (NT, ((), ())), preferred_element_type=f32)
                q = q + lax.dot_general(own, w[1], (NT, ((), ())), preferred_element_type=f32)
            else:
                q = product(halves(own), w, NT)
            out_ref[:, cut(k)] = (q * scale).astype(out_ref.dtype)
            if not last:
                r_ref[:, cut(k)] = q

        def trail(i, low, k=k):
            wide = slice(low * TILE, rank)
            a = (uh_ref[cut(k), cut(i)], ul_ref[cut(k), cut(i)])
            b = (uh_ref[cut(k), wide], ul_ref[cut(k), wide])
            a_ref[cut(i), wide] = a_ref[cut(i), wide] - product(a, b, TN)

        def carry(i, k=k):
            u = (uh_ref[cut(k), cut(i)], ul_ref[cut(k), cut(i)])
            own = s_ref[:, cut(i)].astype(f32) if k == 0 else r_ref[:, cut(i)]
            r_ref[:, cut(i)] = own - product(halves(r_ref[:, cut(k)]), u, NN)

        if last:
            solve()
        else:
            if k + 2 < tiles:
                aside.append(spread)
                aside.append(functools.partial(trail, k + 1, k + 2))
            for i in range(k + 2, tiles):
                aside.append(functools.partial(trail, i, i))
            aside.append(solve)
            for i in range(k + 1, tiles):
                aside.append(functools.partial(carry, i))


def whiten(gram, s, scale):
    rows, rank = s.shape
    return pl.pallas_call(
        functools.partial(whiten_kernel, scale),
        out_shape=jax.ShapeDtypeStruct((rows, rank), bf16),
        scratch_shapes=[
            pltpu.VMEM((rank, rank), f32),
            pltpu.VMEM((rows, rank), f32),
            pltpu.VMEM((TILE, 2 * TILE), f32),
            pltpu.VMEM((TILE, TILE), f32),
            pltpu.VMEM((2 * PANEL * PANEL + PANEL, TILE), f32),
            pltpu.VMEM((rank, rank), bf16),
            pltpu.VMEM((rank, rank), bf16),
        ],
        compiler_params=pltpu.CompilerParams(vmem_limit_bytes=32 * 1024 * 1024),
    )(gram, s)


AXES = ("dir", "z", "y", "core")
PLANE = ("core", "dir", "y")


def scales_of(exponent_table):
    total = jnp.zeros(exponent_table.shape, jnp.float32)
    for exponent_value in range(-2, 3):
        total = total + jnp.where(
            exponent_table == exponent_value, jnp.float32(2.0**exponent_value), jnp.float32(0.0)
        )
    return total.astype(jnp.bfloat16)


def dequantize(values, exponent_table):
    height, breadth = values.shape
    edge_rows = height // exponent_table.shape[0]
    edge_cols = breadth // exponent_table.shape[1]
    scale_table = scales_of(exponent_table)
    tiled = values.reshape(exponent_table.shape[0], edge_rows, exponent_table.shape[1], edge_cols)
    tiled = tiled * scale_table[:, None, :, None]
    return tiled.reshape(height, breadth)


def listed(axes, sizes, shifts):
    names = tuple(sizes)
    ids = np.arange(math.prod(sizes.values())).reshape(tuple(sizes.values()))
    for name, shift in shifts.items():
        ids = np.roll(ids, -shift, axis=names.index(name))
    kept = [names.index(name) for name in names if name not in axes]
    ids = ids.transpose(kept + [names.index(name) for name in axes])
    width = math.prod(sizes[name] for name in axes)
    return [[int(i) for i in group] for group in ids.reshape(-1, width)]


def from_the_ends(group):
    half = len(group) // 2
    pairs = zip(group[half:], group[:half][::-1])
    return group[:1] + [device for pair in pairs for device in pair][:-1]


def exchange(pieces, groups):
    shape = pieces.shape
    paired = pieces.reshape(len(groups[0]), -1, 2, TILE)
    return lax.all_to_all(paired, AXES, 0, 0, axis_index_groups=groups).reshape(shape)


def sum_and_copy(pieces, count, copies):
    size = pieces.shape[0] // count
    chooser = jnp.asarray(np.tile(np.eye(size), (copies, count)), jnp.bfloat16)
    return jnp.dot(chooser, pieces, preferred_element_type=jnp.float32).astype(jnp.bfloat16)


def body(slab, exponents, sketch):
    scaled_values = dequantize(slab, exponents)
    partial_values = jnp.dot(scaled_values, sketch, preferred_element_type=jnp.float32)
    dirs, planes, depth = (lax.axis_size(axes) for axes in ("dir", PLANE, "z"))
    rank = sketch.shape[1]
    parts = partial_values.astype(jnp.bfloat16).reshape(dirs, -1, rank)
    sizes = {name: lax.axis_size(name) for name in AXES}
    middle = {name: sizes[name] // 2 for name in AXES[:-1]}
    parts = jnp.roll(parts, -middle["dir"], axis=0)
    row = listed(("dir",), sizes, {"dir": middle["dir"]})
    parts = lax.all_to_all(parts, AXES, 0, 0, axis_index_groups=row)

    tiles = rank // TILE
    distinct = tiles * tiles // 2 * TILE + tiles // 2
    height = -(-distinct // (2 * planes)) * 2 * planes
    sketched, gram = local_gram(parts, height)
    flat = listed(PLANE, sizes, {"dir": middle["dir"], "y": middle["y"], "core": 1})
    upright = listed(("z",), sizes, {"z": middle["z"]})
    upright = [from_the_ends(group) for group in upright]
    gram = exchange(gram, flat)
    gram = exchange(sum_and_copy(gram, planes, depth), upright)
    gram = exchange(sum_and_copy(gram, depth, planes), flat)
    texel_count = sketched.shape[0] * planes * depth
    return whiten(gram, sketched, math.sqrt(texel_count))


def solution(mesh):
    fine = Mesh(mesh.devices.reshape(4, 16, 4, 2), ("dir", "z", "y", "core"))
    tex = ("z", "y", "core")
    return jax.shard_map(
        body,
        mesh=fine,
        in_specs=(P(tex, "dir"), P(tex, "dir"), P("dir", None)),
        out_specs=P(tex + ("dir",), None),
        check_vma=False,
    )
```
